32 devices in a mesh: depth: 2 (over x), strip: 16 (over z, y, core).
Axes of the slice: x: 2, y: 2, z: 4, core: 2. Of those that a mesh axis runs over, the one named last changes fastest.
Arguments:
- surface: float32 [2, 4, 256, 1024], P(None, None, 'strip'), may hold values from -6 to 6
- velocity_class: int32 [2, 256, 1024], P('depth', 'strip'), may hold values from 0 to 7
- table: float32 [2, 8, 2, 10], replicated, may hold values from -2 to 2
Outputs:
- image: float32 [2, 256, 1024], P('depth', 'strip')
The draws below stay inside these ranges and needn't reach their ends.
All inputs are finite; a program needn't handle non-finite values.
Results may differ from the reference program's by a relative error of at most 0.00017.
Values sent between devices are 32-bit elements; how exact they have to be, the bound alone decides.
A program may use at most 64 MiB of HBM per device.

```python
import math
import jax
import jax.numpy as jnp

NY = 1024
FREQS = 2
PASSES = 9
CLASSES = 8
TERMS = 10
NX = 256
DEPTHS = 2


def draw_table(key, part):
    theta_key = jax.random.fold_in(key, 11)
    radius_key = jax.random.fold_in(key, 12)
    theta = jnp.exp(jax.random.uniform(theta_key, (FREQS, CLASSES), jnp.float32, math.log(2.0), math.log(6.0)))
    radius = jax.random.uniform(radius_key, (FREQS, CLASSES), jnp.float32, 0.85, 1.0)
    node_angle = (jnp.arange(64, dtype=jnp.float32) + 0.5) * (math.pi / 64.0)
    phase = theta[:, :, None] * jnp.cos(node_angle)[None, None, :]
    real_value = radius[:, :, None] * jnp.cos(phase)
    imag_value = radius[:, :, None] * jnp.sin(phase)
    degrees = jnp.arange(TERMS, dtype=jnp.float32)
    basis = jnp.cos(degrees[:, None] * node_angle[None, :]) * jnp.where(degrees == 0, 1.0, 2.0)[:, None] / 64.0
    real_coef = jnp.einsum('fcm,km->fck', real_value, basis)
    imag_coef = jnp.einsum('fcm,km->fck', imag_value, basis)
    return jnp.stack([real_coef, imag_coef], axis=2).astype(jnp.float32)


def touch_ends(entries, key, low, top_value):
    longest = entries.shape.index(max(entries.shape))
    spots = []
    for shift in (0, 1):
        where = [jax.random.randint(jax.random.fold_in(key, axis), (), 0, length) for axis, length in enumerate(entries.shape)]
        where[longest] = (where[longest] + shift) % entries.shape[longest]
        spots.append(tuple(where))
    return entries.at[spots[0]].set(low).at[spots[1]].set(top_value)


def steps_of(key, dims, pieces, least, largest):
    factor_of, own = 1.0, jax.random.fold_in(key, 6)
    for dim, blocks in pieces:
        draws = jnp.exp(jax.random.uniform(jax.random.fold_in(own, dim), (blocks,), jnp.float32, least / len(pieces), largest / len(pieces)))
        factor_of = factor_of * jnp.repeat(draws, dims[dim] // blocks).reshape([-1 if axis == dim else 1 for axis in range(len(dims))])
    return factor_of


def scatter_about(rng, dims, scale, limit, cuts=(), kind=jnp.bfloat16):
    loudness = steps_of(rng, dims, cuts, -0.22, 0.18) if cuts else 1.0
    entries = jax.random.normal(rng, dims, jnp.float32) * scale * loudness
    return jnp.minimum(jnp.maximum(entries, -limit), limit).astype(kind)


def setup_inputs(seed: int = 0) -> dict:
    streams_of = jax.random.split(jax.random.key(seed), 4)
    surface = scatter_about(streams_of[0], (FREQS, 4, NX, NY), 1.0, 6.0, ((2, 16),), jnp.float32)
    velocity_class = touch_ends(jax.random.randint(streams_of[1], (DEPTHS, NX, NY), 0, CLASSES), jax.random.fold_in(streams_of[1], 1), 0, CLASSES - 1).astype(jnp.int32)
    table = draw_table(jax.random.fold_in(streams_of[3], 71), 0)
    return dict(surface=surface, velocity_class=velocity_class, table=table)


def mcclellan(field):
    lead = [(0, 0)] * (field.ndim - 2)
    padded = jnp.pad(field, lead + [(1, 1), (1, 1)])
    beside = padded[..., 2:, 1:-1] + padded[..., :-2, 1:-1] + padded[..., 1:-1, 2:] + padded[..., 1:-1, :-2]
    corners = padded[..., 2:, 2:] + padded[..., 2:, :-2] + padded[..., :-2, 2:] + padded[..., :-2, :-2]
    return -0.5 * field + 0.25 * beside + 0.125 * corners


def weigh(result, field, real_part, imag_part):
    return jnp.stack([
        result[:, 0] + (real_part * field[:, 0] - imag_part * field[:, 1]),
        result[:, 1] + (real_part * field[:, 1] + imag_part * field[:, 0]),
        result[:, 2] + (real_part * field[:, 2] + imag_part * field[:, 3]),
        result[:, 3] + (real_part * field[:, 3] - imag_part * field[:, 2])], axis=1)


def correlate(fields):
    total = jnp.zeros(fields.shape[2:], jnp.float32)
    for freq_index in range(fields.shape[0]):
        total = total + (fields[freq_index, 0] * fields[freq_index, 2] + fields[freq_index, 1] * fields[freq_index, 3])
    return total


def reference(surface, velocity_class, table):
    fields = surface
    images = []
    for level_index in range(velocity_class.shape[0]):
        classes_here = velocity_class[level_index]
        pairs = [table[:, :, :, degree][:, classes_here] for degree in range(PASSES + 1)]
        result = weigh(jnp.zeros_like(fields), fields, pairs[0][..., 0], pairs[0][..., 1])
        previous, current = fields, fields
        for degree in range(PASSES):
            if degree == 0:
                following = mcclellan(current)
            else:
                following = 2.0 * mcclellan(current) - previous
            previous, current = current, following
            result = weigh(result, current, pairs[degree + 1][..., 0], pairs[degree + 1][..., 1])
        fields = result
        images.append(correlate(fields))
    return jnp.stack(images)
```

```python
import functools

import jax
import jax.numpy as jnp
from jax import lax
from jax.experimental import pallas as pl
from jax.experimental.pallas import tpu as pltpu
from jax.sharding import PartitionSpec as P

PASSES = 9
CLASSES = 8
LANES = 128
SUBLANES = 8
MESH = pl.DeviceIdType.MESH


def extended(shard, sides, width):
    for axis, dim in sides:
        devices, length = (lax.axis_size(axis), shard.shape[dim])
        up = [(i, (i + 1) % devices) for i in range(devices - 1)]
        down = [(j, i) for i, j in up]
        last = lax.slice_in_dim(shard, length - width, length, axis=dim)
        initial = lax.slice_in_dim(shard, 0, width, axis=dim)
        before = lax.ppermute(last, axis, up)
        after = lax.ppermute(initial, axis, down)
        shard = jnp.concatenate([before, shard, after], axis=dim)
    return shard


def mcclellan(field):
    lead = [(0, 0)] * (field.ndim - 2)
    padded = jnp.pad(field, lead + [(1, 1), (1, 1)])
    beside = (
        padded[..., 2:, 1:-1]
        + padded[..., :-2, 1:-1]
        + padded[..., 1:-1, 2:]
        + padded[..., 1:-1, :-2]
    )
    corners = (
        padded[..., 2:, 2:] + padded[..., 2:, :-2] + padded[..., :-2, 2:] + padded[..., :-2, :-2]
    )
    return -0.5 * field + 0.25 * beside + 0.125 * corners


def weigh(result, field, real_part, imag_part):
    return jnp.stack(
        [
            result[:, 0] + (real_part * field[:, 0] - imag_part * field[:, 1]),
            result[:, 1] + (real_part * field[:, 1] + imag_part * field[:, 0]),
            result[:, 2] + (real_part * field[:, 2] + imag_part * field[:, 3]),
            result[:, 3] + (real_part * field[:, 3] - imag_part * field[:, 2]),
        ],
        axis=1,
    )


def correlate(fields):
    total = jnp.zeros(fields.shape[2:], jnp.float32)
    for freq_index in range(fields.shape[0]):
        total = total + (
            fields[freq_index, 0] * fields[freq_index, 2]
            + fields[freq_index, 1] * fields[freq_index, 3]
        )
    return total


def tile_halo(sending, rim_width):
    return extended(sending, (("depth", 4), ("strip", 3)), rim_width)


def clip_domain(field, rim_width):
    row_count = field.shape[-2] - 2 * rim_width
    row_ids = (
        lax.axis_index("strip") * row_count
        - rim_width
        + jnp.arange(field.shape[-2], dtype=jnp.int32)
    )
    keep = ((row_ids >= 0) & (row_ids < row_count * lax.axis_size("strip")))[:, None]
    col_count = field.shape[-1] - 2 * rim_width
    col_ids = (
        lax.axis_index("depth") * col_count
        - rim_width
        + jnp.arange(field.shape[-1], dtype=jnp.int32)
    )
    keep = keep & ((col_ids >= 0) & (col_ids < col_count * lax.axis_size("depth")))[None, :]
    return jnp.where(keep, field, 0.0)


def chebyshev(fields, onehot, table_part, rim_width, widen):
    row_count = fields.shape[-2]
    col_count = fields.shape[-1]

    def coefficients(degree):
        pair = jnp.einsum(
            "cij,fcp->fpij", onehot, table_part[:, :, :, degree], precision=lax.Precision.HIGHEST
        )
        return (pair[:, 0], pair[:, 1])

    real_part, imag_part = coefficients(0)
    result = weigh(jnp.zeros_like(fields), fields, real_part, imag_part)
    sending = fields[None]
    widened = widen(sending, rim_width)
    wide_prev = widened[0]
    wide_curr = widened[-1]
    for inner_pass in range(rim_width):
        degree = inner_pass
        if degree == 0:
            following = mcclellan(wide_curr)
        else:
            following = 2.0 * mcclellan(wide_curr) - wide_prev
        following = clip_domain(following, rim_width)
        wide_prev, wide_curr = (wide_curr, following)
        real_part, imag_part = coefficients(degree + 1)
        inner = wide_curr[..., rim_width : rim_width + row_count, :]
        inner = inner[..., rim_width : rim_width + col_count]
        result = weigh(result, inner, real_part, imag_part)
    return result


def body(surface, velocity_class, table):
    classes = jnp.arange(CLASSES, dtype=jnp.int32)
    rim_width = PASSES
    velocity = lax.all_to_all(velocity_class, "depth", split_axis=2, concat_axis=0, tiled=True)
    col_count = velocity.shape[2]
    fields = lax.dynamic_slice_in_dim(surface, lax.axis_index("depth") * col_count, col_count, 3)

    def descend(level_index, state_pair):
        level_fields, image = state_pair
        classes_here = lax.dynamic_index_in_dim(velocity, level_index, 0, keepdims=False)
        onehot = (classes_here[None] == classes[:, None, None]).astype(jnp.float32)
        level_fields = chebyshev(level_fields, onehot, table, rim_width, tile_halo)
        image = lax.dynamic_update_index_in_dim(image, correlate(level_fields), level_index, 0)
        return (level_fields, image)

    initial = (fields, jnp.zeros((velocity.shape[0], velocity.shape[1], col_count), jnp.float32))
    fields, image = lax.fori_loop(0, velocity.shape[0], descend, initial)
    return lax.all_to_all(image, "depth", split_axis=0, concat_axis=2, tiled=True)


def chunk_of(count):
    for rows in (8, 9, 10, 7, 11, 6, 5, 12, 13, 4, 3, 2):
        if count % rows == 0:
            return rows
    return 1


def column_sum(field, lane):
    tiles = [field[..., i : i + LANES] for i in range(0, field.shape[-1], LANES)]
    turned = [pltpu.roll(t, 1, axis=2) for t in tiles]
    first = lane == 0
    pairs = []
    for i, t in enumerate(tiles):
        before = turned[i - 1] if i else jnp.zeros_like(t)
        pairs.append(t + jnp.where(first, before, turned[i]))
    turned = [pltpu.roll(p, LANES - 1, axis=2) for p in pairs]
    last = lane == LANES - 1
    sums = []
    for i, p in enumerate(pairs):
        after = turned[i + 1] if i + 1 < len(pairs) else tiles[i]
        sums.append(p + jnp.where(last, after, turned[i]))
    return jnp.concatenate(sums, axis=-1)


def migrate(
    strips,
    surface_ref,
    velocity_ref,
    table_ref,
    image_ref,
    base,
    terms,
    paired,
    classes,
    coef,
    part,
    rim_send,
    rim_recv,
    swap_send,
    swap_recv,
):
    rows, full = velocity_ref.shape
    width = base.shape[-1]
    tile = full // 2
    rim = PASSES
    tall = rows + 2 * rim
    step = lax.axis_index("depth")
    strip = lax.axis_index("strip")
    other = 1 - step
    has_up = strip > 0
    has_down = strip < strips - 1
    lane_row = lax.broadcasted_iota(jnp.int32, (SUBLANES, LANES), 1)
    sub = lax.broadcasted_iota(jnp.int32, (SUBLANES, LANES), 0)

    barrier = pltpu.get_barrier_semaphore()
    pl.semaphore_signal(barrier, inc=1, device_id={"depth": other}, device_id_type=MESH)

    @pl.when(has_up)
    def _():
        pl.semaphore_signal(barrier, inc=1, device_id={"strip": strip - 1}, device_id_type=MESH)

    @pl.when(has_down)
    def _():
        pl.semaphore_signal(barrier, inc=1, device_id={"strip": strip + 1}, device_id_type=MESH)

    def window(owner):
        return pl.ds(pl.multiple_of(owner * (full - width), LANES), width)

    for r in range(0, rows, SUBLANES):
        base[0, pl.ds(rim + r, SUBLANES)] = jnp.swapaxes(
            surface_ref[:, pl.ds(r, SUBLANES), window(step)], 0, 1
        )

    pl.semaphore_wait(barrier, 1 + has_up.astype(jnp.int32) + has_down.astype(jnp.int32))

    def rims(level):
        up = pltpu.make_async_remote_copy(
            src_ref=base.at[level, pl.ds(rim, rim)],
            dst_ref=base.at[level, pl.ds(rim + rows, rim)],
            send_sem=rim_send.at[level, 0],
            recv_sem=rim_recv.at[level, 0],
            device_id={"strip": strip - 1},
            device_id_type=MESH,
        )
        down = pltpu.make_async_remote_copy(
            src_ref=base.at[level, pl.ds(rows, rim)],
            dst_ref=base.at[level, pl.ds(0, rim)],
            send_sem=rim_send.at[level, 1],
            recv_sem=rim_recv.at[level, 1],
            device_id={"strip": strip + 1},
            device_id_type=MESH,
        )
        return up, down

    def start_rims(level):
        up, down = rims(level)
        pl.when(has_up)(up.start)
        pl.when(has_down)(down.start)

    def zero_rims(level):
        @pl.when(jnp.logical_not(has_up))
        def _():
            base[level, pl.ds(0, rim)] = jnp.zeros((rim, SUBLANES, width), jnp.float32)

        @pl.when(jnp.logical_not(has_down))
        def _():
            base[level, pl.ds(rim + rows, rim)] = jnp.zeros((rim, SUBLANES, width), jnp.float32)

    def await_rims(level):
        up, down = rims(level)
        pl.when(has_down)(up.wait_recv)
        pl.when(has_up)(down.wait_recv)

    def end_rims(level):
        up, down = rims(level)
        pl.when(has_up)(up.wait_send)
        pl.when(has_down)(down.wait_send)

    start_rims(0)
    swap_classes = pltpu.make_async_remote_copy(
        src_ref=velocity_ref.at[:, window(other)],
        dst_ref=classes.at[step],
        send_sem=swap_send.at[0],
        recv_sem=swap_recv.at[0],
        device_id={"depth": other},
        device_id_type=MESH,
    )
    swap_classes.start()
    classes[step] = velocity_ref[:, window(step)]
    zero_rims(0)

    low_half = sub < SUBLANES // 2
    quarter = lax.rem(sub, 4)
    sign = jnp.where((quarter == 1) | (quarter == 2), -1.0, 1.0)

    def fill(degree, carry):
        for p in range(2):
            spread = jnp.zeros((SUBLANES, LANES), jnp.float32)
            for c in range(CLASSES):
                value = jnp.where(low_half, table_ref[0, c, p, degree], table_ref[1, c, p, degree])
                spread = jnp.where(lane_row == c, value, spread)
            coef[p, degree] = spread * sign if p else spread
        return carry

    lax.fori_loop(0, PASSES + 1, fill, 0)

    swap_classes.wait_recv()
    tiles = range(0, width, LANES)

    def weigh_row(level, r):
        kind = classes[level, pl.ds(r, 1), :]
        swapped = lax.rem(sub, 2) == 0
        out = []
        for i in tiles:
            index = jnp.broadcast_to(kind[:, i : i + LANES], (SUBLANES, LANES))
            same = cross = None
            for k in range(PASSES + 1):
                if k == 0:
                    term = base[level, rim + r, :, i : i + LANES]
                else:
                    term = terms[k - 1, rim + r, :, i : i + LANES]
                real = jnp.take_along_axis(coef[0, k], index, axis=1) * term
                imag = jnp.take_along_axis(coef[1, k], index, axis=1) * term
                same = real if same is None else same + real
                cross = imag if cross is None else cross + imag
            cross = jnp.where(
                swapped, pltpu.roll(cross, SUBLANES - 1, axis=0), pltpu.roll(cross, 1, axis=0)
            )
            out.append(same + cross)
        return jnp.concatenate(out, axis=-1)

    def image_row(level, value, r):
        kept = lax.rem(lax.broadcasted_iota(jnp.int32, value.shape, 0), 4) >= 2
        product = jnp.where(kept, value * pltpu.roll(value, 2, axis=0), 0.0)
        part[level, pl.ds(r, 1), :] = jnp.sum(product, axis=0, keepdims=True)

    for level in range(2):
        await_rims(level)
        for degree in range(1, PASSES + 1):
            count = tall - 2 * degree
            chunk = chunk_of(count)

            def advance(i, carry, degree=degree, chunk=chunk):
                at = degree + i * chunk
                if degree == 1:
                    field = base[level, pl.ds(at - 1, chunk + 2)]
                else:
                    field = terms[degree - 2, pl.ds(at - 1, chunk + 2)]
                pair = field[:-1] + field[1:]
                lane = lax.broadcasted_iota(jnp.int32, (chunk, SUBLANES, LANES), 2)
                spread = column_sum(pair[:-1] + pair[1:], lane)
                if degree == 1:
                    joint = 0.125 * spread
                else:
                    joint = 0.25 * spread - paired[pl.ds(at, chunk)]
                if degree < PASSES:
                    paired[pl.ds(at, chunk)] = joint
                terms[degree - 1, pl.ds(at, chunk)] = joint - field[1:-1]
                return carry

            lax.fori_loop(0, count // chunk, advance, 0)
            if degree < PASSES:

                @pl.when(jnp.logical_not(has_up))
                def _():
                    terms[degree - 1, rim - 1] = jnp.zeros((SUBLANES, width), jnp.float32)

                @pl.when(jnp.logical_not(has_down))
                def _():
                    terms[degree - 1, rim + rows] = jnp.zeros((SUBLANES, width), jnp.float32)

        def weigh(r, carry):
            value = weigh_row(level, r)
            if level == 0:
                base[1, rim + r] = value
            image_row(level, value, r)
            return carry

        lax.fori_loop(0, rows, weigh, 0)
        if level == 0:
            start_rims(1)
            zero_rims(1)
        here = pl.ds(pl.multiple_of(step * tile, LANES), tile)
        inner = pl.ds(pl.multiple_of(step * (width - tile), LANES), tile)

        @pl.when(step == level)
        def _():
            image_ref[:, here] = part[level, :, inner]

        @pl.when(step != level)
        def _():
            pltpu.make_async_remote_copy(
                src_ref=part.at[level, :, inner],
                dst_ref=image_ref.at[:, here],
                send_sem=swap_send.at[1],
                recv_sem=swap_recv.at[1],
                device_id={"depth": other},
                device_id_type=MESH,
            ).start()

    there = pl.ds(pl.multiple_of(other * tile, LANES), tile)
    inner = pl.ds(pl.multiple_of(step * (width - tile), LANES), tile)
    swap_image = pltpu.make_async_remote_copy(
        src_ref=part.at[0, :, inner],
        dst_ref=image_ref.at[:, there],
        send_sem=swap_send.at[1],
        recv_sem=swap_recv.at[1],
        device_id={"depth": other},
        device_id_type=MESH,
    )
    swap_image.wait_recv()
    swap_image.wait_send()
    swap_classes.wait_send()
    end_rims(0)
    end_rims(1)


def in_kernel(strips, surface, velocity_class, table):
    freqs, parts, rows, full = surface.shape
    width = full // 2 + LANES
    tall = rows + 2 * PASSES
    f32 = jnp.float32
    return pl.pallas_call(
        functools.partial(migrate, strips),
        out_shape=jax.ShapeDtypeStruct((rows, full), f32),
        in_specs=[
            pl.BlockSpec(memory_space=pltpu.VMEM),
            pl.BlockSpec(memory_space=pltpu.VMEM),
            pl.BlockSpec(memory_space=pltpu.SMEM),
        ],
        out_specs=pl.BlockSpec(memory_space=pltpu.VMEM),
        scratch_shapes=[
            pltpu.VMEM((2, tall, SUBLANES, width), f32),
            pltpu.VMEM((PASSES, tall, SUBLANES, width), f32),
            pltpu.VMEM((tall, SUBLANES, width), f32),
            pltpu.VMEM((2, rows, width), jnp.int32),
            pltpu.VMEM((2, PASSES + 1, SUBLANES, LANES), f32),
            pltpu.VMEM((2, rows, width), f32),
            pltpu.SemaphoreType.DMA((2, 2)),
            pltpu.SemaphoreType.DMA((2, 2)),
            pltpu.SemaphoreType.DMA((2,)),
            pltpu.SemaphoreType.DMA((2,)),
        ],
        compiler_params=pltpu.CompilerParams(
            collective_id=0, has_side_effects=True, vmem_limit_bytes=40 * 2**20
        ),
    )(
        surface.reshape(freqs * parts, rows, full),
        velocity_class.reshape(rows, full),
        table,
    )[None]


def fits(mesh, surface, velocity_class):
    freqs, parts, rows, full = surface.shape
    return (
        mesh.shape["depth"] == 2
        and velocity_class.shape[0] == 1
        and freqs * parts == SUBLANES
        and rows % SUBLANES == 0
        and rows >= PASSES
        and full % (2 * LANES) == 0
        and 2 * PASSES <= LANES <= full // 2
        and rows * full <= 2**15
    )


def solution(mesh):
    in_specs = (P(None, None, "strip", None), P("depth", "strip", None), P())
    out_specs = P("depth", "strip", None)

    def part(surface, velocity_class, table):
        if fits(mesh, surface, velocity_class):
            return in_kernel(mesh.shape["strip"], surface, velocity_class, table)
        return body(surface, velocity_class, table)

    return jax.shard_map(part, mesh=mesh, in_specs=in_specs, out_specs=out_specs, check_vma=False)
```

```python
import functools

import jax
import jax.numpy as jnp
from jax import lax
from jax.experimental import pallas as pl
from jax.experimental.pallas import tpu as pltpu
from jax.sharding import PartitionSpec as P

PASSES = 9
CLASSES = 8
LANES = 128
SUBLANES = 8
MESH = pl.DeviceIdType.MESH


def extended(shard, sides, width):
    for axis, dim in sides:
        devices, length = (lax.axis_size(axis), shard.shape[dim])
        up = [(i, (i + 1) % devices) for i in range(devices - 1)]
        down = [(j, i) for i, j in up]
        last = lax.slice_in_dim(shard, length - width, length, axis=dim)
        initial = lax.slice_in_dim(shard, 0, width, axis=dim)
        before = lax.ppermute(last, axis, up)
        after = lax.ppermute(initial, axis, down)
        shard = jnp.concatenate([before, shard, after], axis=dim)
    return shard


def mcclellan(field):
    lead = [(0, 0)] * (field.ndim - 2)
    padded = jnp.pad(field, lead + [(1, 1), (1, 1)])
    beside = (
        padded[..., 2:, 1:-1]
        + padded[..., :-2, 1:-1]
        + padded[..., 1:-1, 2:]
        + padded[..., 1:-1, :-2]
    )
    corners = (
        padded[..., 2:, 2:] + padded[..., 2:, :-2] + padded[..., :-2, 2:] + padded[..., :-2, :-2]
    )
    return -0.5 * field + 0.25 * beside + 0.125 * corners


def weigh(result, field, real_part, imag_part):
    return jnp.stack(
        [
            result[:, 0] + (real_part * field[:, 0] - imag_part * field[:, 1]),
            result[:, 1] + (real_part * field[:, 1] + imag_part * field[:, 0]),
            result[:, 2] + (real_part * field[:, 2] + imag_part * field[:, 3]),
            result[:, 3] + (real_part * field[:, 3] - imag_part * field[:, 2]),
        ],
        axis=1,
    )


def correlate(fields):
    total = jnp.zeros(fields.shape[2:], jnp.float32)
    for freq_index in range(fields.shape[0]):
        total = total + (
            fields[freq_index, 0] * fields[freq_index, 2]
            + fields[freq_index, 1] * fields[freq_index, 3]
        )
    return total


def tile_halo(sending, rim_width):
    return extended(sending, (("depth", 4), ("strip", 3)), rim_width)


def clip_domain(field, rim_width):
    row_count = field.shape[-2] - 2 * rim_width
    row_ids = (
        lax.axis_index("strip") * row_count
        - rim_width
        + jnp.arange(field.shape[-2], dtype=jnp.int32)
    )
    keep = ((row_ids >= 0) & (row_ids < row_count * lax.axis_size("strip")))[:, None]
    col_count = field.shape[-1] - 2 * rim_width
    col_ids = (
        lax.axis_index("depth") * col_count
        - rim_width
        + jnp.arange(field.shape[-1], dtype=jnp.int32)
    )
    keep = keep & ((col_ids >= 0) & (col_ids < col_count * lax.axis_size("depth")))[None, :]
    return jnp.where(keep, field, 0.0)


def chebyshev(fields, onehot, table_part, rim_width, widen):
    row_count = fields.shape[-2]
    col_count = fields.shape[-1]

    def coefficients(degree):
        pair = jnp.einsum(
            "cij,fcp->fpij", onehot, table_part[:, :, :, degree], precision=lax.Precision.HIGHEST
        )
        return (pair[:, 0], pair[:, 1])

    real_part, imag_part = coefficients(0)
    result = weigh(jnp.zeros_like(fields), fields, real_part, imag_part)
    sending = fields[None]
    widened = widen(sending, rim_width)
    wide_prev = widened[0]
    wide_curr = widened[-1]
    for inner_pass in range(rim_width):
        degree = inner_pass
        if degree == 0:
            following = mcclellan(wide_curr)
        else:
            following = 2.0 * mcclellan(wide_curr) - wide_prev
        following = clip_domain(following, rim_width)
        wide_prev, wide_curr = (wide_curr, following)
        real_part, imag_part = coefficients(degree + 1)
        inner = wide_curr[..., rim_width : rim_width + row_count, :]
        inner = inner[..., rim_width : rim_width + col_count]
        result = weigh(result, inner, real_part, imag_part)
    return result


def body(surface, velocity_class, table):
    classes = jnp.arange(CLASSES, dtype=jnp.int32)
    rim_width = PASSES
    velocity = lax.all_to_all(velocity_class, "depth", split_axis=2, concat_axis=0, tiled=True)
    col_count = velocity.shape[2]
    fields = lax.dynamic_slice_in_dim(surface, lax.axis_index("depth") * col_count, col_count, 3)

    def descend(level_index, state_pair):
        level_fields, image = state_pair
        classes_here = lax.dynamic_index_in_dim(velocity, level_index, 0, keepdims=False)
        onehot = (classes_here[None] == classes[:, None, None]).astype(jnp.float32)
        level_fields = chebyshev(level_fields, onehot, table, rim_width, tile_halo)
        image = lax.dynamic_update_index_in_dim(image, correlate(level_fields), level_index, 0)
        return (level_fields, image)

    initial = (fields, jnp.zeros((velocity.shape[0], velocity.shape[1], col_count), jnp.float32))
    fields, image = lax.fori_loop(0, velocity.shape[0], descend, initial)
    return lax.all_to_all(image, "depth", split_axis=0, concat_axis=2, tiled=True)


def column_sum(tiles, lane, sub):
    lower = sub < SUBLANES // 2
    turned = [pltpu.roll(t, 1, axis=2) for t in tiles]
    before = jnp.where(lower, 0.0, pltpu.roll(turned[-1], SUBLANES // 2, axis=1))
    pairs = []
    for t, now in zip(tiles, turned):
        pairs.append(t + jnp.where(lane == 0, before, now))
        before = now
    turned = [pltpu.roll(p, LANES - 1, axis=2) for p in pairs]
    after = jnp.where(lower, pltpu.roll(turned[0], SUBLANES // 2, axis=1), tiles[-1])
    sums = []
    for p, now in zip(pairs[::-1], turned[::-1]):
        sums.append(p + jnp.where(lane == LANES - 1, after, now))
        after = now
    return sums[::-1]


def migrate(strips, surface_ref, velocity_ref, table_ref, image_ref, *scratch):
    raw, classes, numbers, coef, spot, part, got, paired = scratch[:8]
    terms = scratch[8 : 9 + PASSES]
    second = scratch[9 + PASSES]
    load_sem, rim_send, rim_recv, swap_send, swap_recv = scratch[10 + PASSES :]
    levels = ((terms[0],) + terms[1:], (second,) + terms[1:])
    results = (second, paired)
    rows, full = velocity_ref.shape
    half = full // 2
    rim = PASSES
    tall = rows + 2 * rim
    step = lax.axis_index("depth")
    strip = lax.axis_index("strip")
    other = 1 - step
    has_up = strip > 0
    has_down = strip < strips - 1
    no_up = jnp.logical_not(has_up)
    no_down = jnp.logical_not(has_down)
    lane = lax.broadcasted_iota(jnp.int32, (SUBLANES, LANES), 1)
    sub = lax.broadcasted_iota(jnp.int32, (SUBLANES, LANES), 0)
    tiles = range(0, half, LANES)

    load_surface = pltpu.make_async_copy(surface_ref.at[step], raw, load_sem.at[0])
    load_classes = pltpu.make_async_copy(velocity_ref, classes.at[step], load_sem.at[1])
    load_table = pltpu.make_async_copy(table_ref, numbers, load_sem.at[2])
    load_surface.start()
    load_classes.start()
    load_table.start()

    barrier = pltpu.get_barrier_semaphore()
    pl.semaphore_signal(barrier, inc=1, device_id={"depth": other}, device_id_type=MESH)

    @pl.when(has_up)
    def _():
        pl.semaphore_signal(barrier, inc=1, device_id={"strip": strip - 1}, device_id_type=MESH)

    @pl.when(has_down)
    def _():
        pl.semaphore_signal(barrier, inc=1, device_id={"strip": strip + 1}, device_id_type=MESH)

    load_surface.wait()
    for r in range(0, rows, SUBLANES):
        for i in tiles:
            block = jnp.concatenate(
                [raw[:, r : r + SUBLANES, i : i + LANES], raw[:, r : r + SUBLANES, half + i : half + i + LANES]],
                axis=0,
            )
            terms[0][rim + r : rim + r + SUBLANES, :, i : i + LANES] = jnp.swapaxes(block, 0, 1)

    load_classes.wait()
    pl.semaphore_wait(barrier, 1 + has_up.astype(jnp.int32) + has_down.astype(jnp.int32))

    def rims(level):
        base = levels[level][0]
        up = pltpu.make_async_remote_copy(
            src_ref=base.at[pl.ds(rim, rim)],
            dst_ref=base.at[pl.ds(rim + rows, rim)],
            send_sem=rim_send.at[level, 0],
            recv_sem=rim_recv.at[level, 0],
            device_id={"strip": strip - 1},
            device_id_type=MESH,
        )
        down = pltpu.make_async_remote_copy(
            src_ref=base.at[pl.ds(rows, rim)],
            dst_ref=base.at[pl.ds(0, rim)],
            send_sem=rim_send.at[level, 1],
            recv_sem=rim_recv.at[level, 1],
            device_id={"strip": strip + 1},
            device_id_type=MESH,
        )
        return up, down

    def start_rims(level):
        up, down = rims(level)
        pl.when(has_up)(up.start)
        pl.when(has_down)(down.start)

    def zero_rims(level):
        base = levels[level][0]

        @pl.when(no_up)
        def _():
            base[:rim] = jnp.zeros((rim, SUBLANES, half), jnp.float32)

        @pl.when(no_down)
        def _():
            base[rim + rows :] = jnp.zeros((rim, SUBLANES, half), jnp.float32)

    def swap_image(level):
        return pltpu.make_async_remote_copy(
            src_ref=part.at[level],
            dst_ref=got,
            send_sem=swap_send.at[1],
            recv_sem=swap_recv.at[1],
            device_id={"depth": other},
            device_id_type=MESH,
        )

    start_rims(0)
    swap_classes = pltpu.make_async_remote_copy(
        src_ref=classes.at[step],
        dst_ref=classes.at[step],
        send_sem=swap_send.at[0],
        recv_sem=swap_recv.at[0],
        device_id={"depth": other},
        device_id_type=MESH,
    )
    swap_classes.start()
    zero_rims(0)

    quarter = lax.rem(sub, 4)
    sign = jnp.where((quarter == 1) | (quarter == 2), -1.0, 1.0)
    load_table.wait()

    def fill(degree, carry):
        for p in range(2):
            spread = jnp.zeros((SUBLANES, LANES), jnp.float32)
            for c in range(CLASSES):
                spread = jnp.where(lane == c, numbers[step, c, p, degree], spread)
            coef[p, degree] = spread * sign if p else spread
        return carry

    lax.fori_loop(0, PASSES + 1, fill, 0)

    def look_up(level):
        def row(r, carry):
            kind = classes[level, pl.ds(r, 1), :]
            for i in tiles:
                index = jnp.where(
                    sub < SUBLANES // 2,
                    jnp.broadcast_to(kind[:, i : i + LANES], (SUBLANES, LANES)),
                    jnp.broadcast_to(kind[:, half + i : half + i + LANES], (SUBLANES, LANES)),
                )
                for p in range(2):
                    for k in range(PASSES + 1):
                        spot[p, k, r, :, i : i + LANES] = jnp.take_along_axis(coef[p, k], index, axis=1)
            return carry

        lax.fori_loop(0, rows, row, 0)

    def weigh(level, low, high):
        held = levels[level]
        even = lax.rem(sub, 2) == 0

        def row(r, carry):
            for i in tiles:
                same = cross = None
                for k in range(PASSES + 1):
                    term = held[k][rim + r, :, i : i + LANES]
                    real = spot[0, k, r, :, i : i + LANES] * term
                    imag = spot[1, k, r, :, i : i + LANES] * term
                    same = real if same is None else same + real
                    cross = imag if cross is None else cross + imag
                cross = jnp.where(
                    even, pltpu.roll(cross, SUBLANES - 1, axis=0), pltpu.roll(cross, 1, axis=0)
                )
                results[level][rim + r, :, i : i + LANES] = same + cross
            return carry

        lax.fori_loop(low, high, row, 0)

    def correlate_step(level):
        for r in range(0, rows, SUBLANES):
            for i in tiles:
                field = results[level][rim + r : rim + r + SUBLANES, :, i : i + LANES]
                field = jnp.swapaxes(field, 0, 1)
                part[level, r : r + SUBLANES, i : i + LANES] = field[0] * field[2] + field[1] * field[3]
                part[level, r : r + SUBLANES, half + i : half + i + LANES] = (
                    field[4] * field[6] + field[5] * field[7]
                )

    def sweep(level, degree, low, high):
        source, target = levels[level][degree - 1], levels[level][degree]
        at = low
        while at < high:
            size = min(3, high - at)
            if high - at == 4:
                size = 2
            lanes = lax.broadcasted_iota(jnp.int32, (size, SUBLANES, LANES), 2)
            subs = lax.broadcasted_iota(jnp.int32, (size, SUBLANES, LANES), 1)
            sums = []
            inner = []
            for i in tiles:
                field = source[at - 1 : at + size + 1, :, i : i + LANES]
                pair = field[:-1] + field[1:]
                sums.append(pair[:-1] + pair[1:])
                inner.append(field[1:-1])
            for i, total, field in zip(tiles, column_sum(sums, lanes, subs), inner):
                if degree == 1:
                    joint = 0.125 * total
                else:
                    joint = 0.25 * total - paired[at : at + size, :, i : i + LANES]
                if degree < PASSES:
                    paired[at : at + size, :, i : i + LANES] = joint
                target[at : at + size, :, i : i + LANES] = joint - field
            at += size

    def inside(level):
        for degree in range(1, PASSES):
            low, high = rim + degree, rim + rows - degree
            if low < high:
                sweep(level, degree, low, high)

    def above(level):
        for degree in range(1, PASSES):
            sweep(level, degree, degree, min(rim + degree, tall // 2))
            @pl.when(no_up)
            def _():
                levels[level][degree][rim - 1] = jnp.zeros((SUBLANES, half), jnp.float32)

    def below(level):
        for degree in range(1, PASSES):
            sweep(level, degree, max(rim + rows - degree, tall // 2), tall - degree)
            @pl.when(no_down)
            def _():
                levels[level][degree][rim + rows] = jnp.zeros((SUBLANES, half), jnp.float32)

    for level in range(2):
        if level == 0:
            swap_classes.wait_recv()
        inside(level)
        look_up(level)
        if level == 1:
            correlate_step(0)

            @pl.when(step == 1)
            def _():
                swap_image(0).start()

        up, down = rims(level)
        pl.when(has_up)(down.wait_recv)
        above(level)
        pl.when(has_down)(up.wait_recv)
        below(level)
        sweep(level, PASSES, rim, rim + rows)
        if level == 0:
            up, down = rims(1)
            weigh(0, 0, rim)
            pl.when(has_up)(up.start)
            weigh(0, rim, rows)
            pl.when(has_down)(down.start)
            zero_rims(1)
        else:
            weigh(1, 0, rows)
            correlate_step(1)

    @pl.when(step == 0)
    def _():
        swap_image(1).start()

    swap = swap_image(0)
    swap.wait_recv()
    image_ref[...] = part[step] + got[...]
    swap.wait_send()
    swap_classes.wait_send()
    for level in range(2):
        up, down = rims(level)
        pl.when(has_up)(up.wait_send)
        pl.when(has_down)(down.wait_send)


def in_kernel(strips, surface, velocity_class, table):
    freqs, parts, rows, full = surface.shape
    half = full // 2
    tall = rows + 2 * PASSES
    f32 = jnp.float32
    fields = pltpu.VMEM((tall, SUBLANES, half), f32)
    return pl.pallas_call(
        functools.partial(migrate, strips),
        out_shape=jax.ShapeDtypeStruct((rows, full), f32),
        in_specs=[pl.BlockSpec(memory_space=pl.ANY)] * 3,
        out_specs=pl.BlockSpec(memory_space=pltpu.VMEM),
        scratch_shapes=[
            pltpu.VMEM((parts, rows, full), f32),
            pltpu.VMEM((2, rows, full), jnp.int32),
            pltpu.SMEM(table.shape, f32),
            pltpu.VMEM((2, PASSES + 1, SUBLANES, LANES), f32),
            pltpu.VMEM((2, PASSES + 1, rows, SUBLANES, half), f32),
            pltpu.VMEM((2, rows, full), f32),
            pltpu.VMEM((rows, full), f32),
        ]
        + [fields] * (PASSES + 3)
        + [
            pltpu.SemaphoreType.DMA((3,)),
            pltpu.SemaphoreType.DMA((2, 2)),
            pltpu.SemaphoreType.DMA((2, 2)),
            pltpu.SemaphoreType.DMA((2,)),
            pltpu.SemaphoreType.DMA((2,)),
        ],
        compiler_params=pltpu.CompilerParams(
            collective_id=0, has_side_effects=True, vmem_limit_bytes=56 * 2**20
        ),
    )(surface, velocity_class.reshape(rows, full), table)[None]


def fits(mesh, surface, velocity_class):
    freqs, parts, rows, full = surface.shape
    return (
        mesh.shape["depth"] == 2
        and velocity_class.shape[0] == 1
        and freqs == 2
        and 2 * parts == SUBLANES
        and rows % SUBLANES == 0
        and PASSES <= rows < 2 * PASSES
        and full % (2 * LANES) == 0
        and rows * full <= 2**15
    )


def solution(mesh):
    in_specs = (P(None, None, "strip", None), P("depth", "strip", None), P())
    out_specs = P("depth", "strip", None)

    def part(surface, velocity_class, table):
        if fits(mesh, surface, velocity_class):
            return in_kernel(mesh.shape["strip"], surface, velocity_class, table)
        return body(surface, velocity_class, table)

    return jax.shard_map(part, mesh=mesh, in_specs=in_specs, out_specs=out_specs, check_vma=False)
```

```python
import functools

import jax
import jax.numpy as jnp
from jax import lax
from jax.experimental import pallas as pl
from jax.experimental.pallas import tpu as pltpu
from jax.sharding import PartitionSpec as P

PASSES = 9
CLASSES = 8
LANES = 128
SUBLANES = 8
MESH = pl.DeviceIdType.MESH


def extended(shard, sides, width):
    for axis, dim in sides:
        devices, length = (lax.axis_size(axis), shard.shape[dim])
        up = [(i, (i + 1) % devices) for i in range(devices - 1)]
        down = [(j, i) for i, j in up]
        last = lax.slice_in_dim(shard, length - width, length, axis=dim)
        initial = lax.slice_in_dim(shard, 0, width, axis=dim)
        before = lax.ppermute(last, axis, up)
        after = lax.ppermute(initial, axis, down)
        shard = jnp.concatenate([before, shard, after], axis=dim)
    return shard


def mcclellan(field):
    lead = [(0, 0)] * (field.ndim - 2)
    padded = jnp.pad(field, lead + [(1, 1), (1, 1)])
    beside = (
        padded[..., 2:, 1:-1]
        + padded[..., :-2, 1:-1]
        + padded[..., 1:-1, 2:]
        + padded[..., 1:-1, :-2]
    )
    corners = (
        padded[..., 2:, 2:] + padded[..., 2:, :-2] + padded[..., :-2, 2:] + padded[..., :-2, :-2]
    )
    return -0.5 * field + 0.25 * beside + 0.125 * corners


def weigh(result, field, real_part, imag_part):
    return jnp.stack(
        [
            result[:, 0] + (real_part * field[:, 0] - imag_part * field[:, 1]),
            result[:, 1] + (real_part * field[:, 1] + imag_part * field[:, 0]),
            result[:, 2] + (real_part * field[:, 2] + imag_part * field[:, 3]),
            result[:, 3] + (real_part * field[:, 3] - imag_part * field[:, 2]),
        ],
        axis=1,
    )


def correlate(fields):
    total = jnp.zeros(fields.shape[2:], jnp.float32)
    for freq_index in range(fields.shape[0]):
        total = total + (
            fields[freq_index, 0] * fields[freq_index, 2]
            + fields[freq_index, 1] * fields[freq_index, 3]
        )
    return total


def tile_halo(sending, rim_width):
    return extended(sending, (("depth", 4), ("strip", 3)), rim_width)


def clip_domain(field, rim_width):
    row_count = field.shape[-2] - 2 * rim_width
    row_ids = (
        lax.axis_index("strip") * row_count
        - rim_width
        + jnp.arange(field.shape[-2], dtype=jnp.int32)
    )
    keep = ((row_ids >= 0) & (row_ids < row_count * lax.axis_size("strip")))[:, None]
    col_count = field.shape[-1] - 2 * rim_width
    col_ids = (
        lax.axis_index("depth") * col_count
        - rim_width
        + jnp.arange(field.shape[-1], dtype=jnp.int32)
    )
    keep = keep & ((col_ids >= 0) & (col_ids < col_count * lax.axis_size("depth")))[None, :]
    return jnp.where(keep, field, 0.0)


def chebyshev(fields, onehot, table_part, rim_width, widen):
    row_count = fields.shape[-2]
    col_count = fields.shape[-1]

    def coefficients(degree):
        pair = jnp.einsum(
            "cij,fcp->fpij", onehot, table_part[:, :, :, degree], precision=lax.Precision.HIGHEST
        )
        return (pair[:, 0], pair[:, 1])

    real_part, imag_part = coefficients(0)
    result = weigh(jnp.zeros_like(fields), fields, real_part, imag_part)
    sending = fields[None]
    widened = widen(sending, rim_width)
    wide_prev = widened[0]
    wide_curr = widened[-1]
    for inner_pass in range(rim_width):
        degree = inner_pass
        if degree == 0:
            following = mcclellan(wide_curr)
        else:
            following = 2.0 * mcclellan(wide_curr) - wide_prev
        following = clip_domain(following, rim_width)
        wide_prev, wide_curr = (wide_curr, following)
        real_part, imag_part = coefficients(degree + 1)
        inner = wide_curr[..., rim_width : rim_width + row_count, :]
        inner = inner[..., rim_width : rim_width + col_count]
        result = weigh(result, inner, real_part, imag_part)
    return result


def body(surface, velocity_class, table):
    classes = jnp.arange(CLASSES, dtype=jnp.int32)
    rim_width = PASSES
    velocity = lax.all_to_all(velocity_class, "depth", split_axis=2, concat_axis=0, tiled=True)
    col_count = velocity.shape[2]
    fields = lax.dynamic_slice_in_dim(surface, lax.axis_index("depth") * col_count, col_count, 3)

    def descend(level_index, state_pair):
        level_fields, image = state_pair
        classes_here = lax.dynamic_index_in_dim(velocity, level_index, 0, keepdims=False)
        onehot = (classes_here[None] == classes[:, None, None]).astype(jnp.float32)
        level_fields = chebyshev(level_fields, onehot, table, rim_width, tile_halo)
        image = lax.dynamic_update_index_in_dim(image, correlate(level_fields), level_index, 0)
        return (level_fields, image)

    initial = (fields, jnp.zeros((velocity.shape[0], velocity.shape[1], col_count), jnp.float32))
    fields, image = lax.fori_loop(0, velocity.shape[0], descend, initial)
    return lax.all_to_all(image, "depth", split_axis=0, concat_axis=2, tiled=True)


def column_sum(tiles, lane, sub):
    lower = sub < SUBLANES // 2
    rights = [pltpu.roll(t, 1, axis=2) for t in tiles]
    lefts = [pltpu.roll(t, LANES - 1, axis=2) for t in tiles]
    before = jnp.where(lower, 0.0, pltpu.roll(rights[-1], SUBLANES // 2, axis=1))
    after = jnp.where(lower, pltpu.roll(lefts[0], SUBLANES // 2, axis=1), 0.0)
    sums = []
    for i, t in enumerate(tiles):
        right = jnp.where(lane == 0, rights[i - 1] if i else before, rights[i])
        left = jnp.where(lane == LANES - 1, lefts[i + 1] if i + 1 < len(tiles) else after, lefts[i])
        sums.append((right + left) + (t + t))
    return sums


def migrate(strips, surface_ref, velocity_ref, table_ref, image_ref, *scratch):
    raw, classes, numbers, coef, spot, part, got, paired = scratch[:8]
    terms = scratch[8 : 9 + PASSES]
    second = scratch[9 + PASSES]
    load_sem, rim_send, rim_recv, swap_send, swap_recv = scratch[10 + PASSES :]
    levels = ((terms[0],) + terms[1:], (second,) + terms[1:])
    results = (second, paired)
    rows, full = velocity_ref.shape
    half = full // 2
    rim = PASSES
    tall = rows + 2 * rim
    step = lax.axis_index("depth")
    strip = lax.axis_index("strip")
    other = 1 - step
    has_up = strip > 0
    has_down = strip < strips - 1
    no_up = jnp.logical_not(has_up)
    no_down = jnp.logical_not(has_down)
    lane = lax.broadcasted_iota(jnp.int32, (SUBLANES, LANES), 1)
    sub = lax.broadcasted_iota(jnp.int32, (SUBLANES, LANES), 0)
    tiles = range(0, half, LANES)

    load_surface = pltpu.make_async_copy(surface_ref.at[step], raw, load_sem.at[0])
    load_classes = pltpu.make_async_copy(velocity_ref, classes.at[step], load_sem.at[1])
    load_table = pltpu.make_async_copy(table_ref, numbers, load_sem.at[2])
    load_surface.start()
    load_classes.start()
    load_table.start()

    barrier = pltpu.get_barrier_semaphore()
    pl.semaphore_signal(barrier, inc=1, device_id={"depth": other}, device_id_type=MESH)

    @pl.when(has_up)
    def _():
        pl.semaphore_signal(barrier, inc=1, device_id={"strip": strip - 1}, device_id_type=MESH)

    @pl.when(has_down)
    def _():
        pl.semaphore_signal(barrier, inc=1, device_id={"strip": strip + 1}, device_id_type=MESH)

    load_surface.wait()
    for r in range(0, rows, SUBLANES):
        for i in tiles:
            block = jnp.concatenate(
                [raw[:, r : r + SUBLANES, i : i + LANES], raw[:, r : r + SUBLANES, half + i : half + i + LANES]],
                axis=0,
            )
            terms[0][rim + r : rim + r + SUBLANES, :, i : i + LANES] = jnp.swapaxes(block, 0, 1)

    load_classes.wait()
    pl.semaphore_wait(barrier, 1 + has_up.astype(jnp.int32) + has_down.astype(jnp.int32))

    def rims(level):
        base = levels[level][0]
        up = pltpu.make_async_remote_copy(
            src_ref=base.at[pl.ds(rim, rim)],
            dst_ref=base.at[pl.ds(rim + rows, rim)],
            send_sem=rim_send.at[level, 0],
            recv_sem=rim_recv.at[level, 0],
            device_id={"strip": strip - 1},
            device_id_type=MESH,
        )
        down = pltpu.make_async_remote_copy(
            src_ref=base.at[pl.ds(rows, rim)],
            dst_ref=base.at[pl.ds(0, rim)],
            send_sem=rim_send.at[level, 1],
            recv_sem=rim_recv.at[level, 1],
            device_id={"strip": strip + 1},
            device_id_type=MESH,
        )
        return up, down

    def start_rims(level):
        up, down = rims(level)
        pl.when(has_up)(up.start)
        pl.when(has_down)(down.start)

    def zero_rims(level):
        base = levels[level][0]

        @pl.when(no_up)
        def _():
            base[:rim] = jnp.zeros((rim, SUBLANES, half), jnp.float32)

        @pl.when(no_down)
        def _():
            base[rim + rows :] = jnp.zeros((rim, SUBLANES, half), jnp.float32)

    def swap_image(level, piece):
        here = pl.ds(piece * (rows // 2), rows // 2)
        return pltpu.make_async_remote_copy(
            src_ref=part.at[level, here],
            dst_ref=got.at[here],
            send_sem=swap_send.at[1 + piece],
            recv_sem=swap_recv.at[1 + piece],
            device_id={"depth": other},
            device_id_type=MESH,
        )

    start_rims(0)
    swap_classes = pltpu.make_async_remote_copy(
        src_ref=classes.at[step],
        dst_ref=classes.at[step],
        send_sem=swap_send.at[0],
        recv_sem=swap_recv.at[0],
        device_id={"depth": other},
        device_id_type=MESH,
    )
    swap_classes.start()
    zero_rims(0)

    quarter = lax.rem(sub, 4)
    sign = jnp.where((quarter == 1) | (quarter == 2), -1.0, 1.0)
    load_table.wait()

    def fill(degree, carry):
        for p in range(2):
            spread = jnp.zeros((SUBLANES, LANES), jnp.float32)
            for c in range(CLASSES):
                spread = jnp.where(lane == c, numbers[step, c, p, degree], spread)
            coef[p, degree] = spread * sign if p else spread
        return carry

    lax.fori_loop(0, PASSES + 1, fill, 0)

    def look_up(level):
        def block(b, carry):
            for j in range(4):
                r = b * 4 + j
                kind = classes[level, pl.ds(r, 1), :]
                for i in tiles:
                    index = jnp.where(
                        sub < SUBLANES // 2,
                        jnp.broadcast_to(kind[:, i : i + LANES], (SUBLANES, LANES)),
                        jnp.broadcast_to(kind[:, half + i : half + i + LANES], (SUBLANES, LANES)),
                    )
                    for p in range(2):
                        for k in range(PASSES + 1):
                            spot[p, k, r, :, i : i + LANES] = jnp.take_along_axis(
                                coef[p, k], index, axis=1, mode="promise_in_bounds"
                            )
            return carry

        lax.fori_loop(0, rows // 4, block, 0)

    def weigh(level, low, high):
        held = levels[level]
        for r in range(low, high, 4):
            size = min(4, high - r)
            even = lax.rem(lax.broadcasted_iota(jnp.int32, (size, SUBLANES, LANES), 1), 2) == 0
            for i in tiles:
                same = cross = None
                for k in range(PASSES + 1):
                    term = held[k][rim + r : rim + r + size, :, i : i + LANES]
                    real = spot[0, k, r : r + size, :, i : i + LANES] * term
                    imag = spot[1, k, r : r + size, :, i : i + LANES] * term
                    same = real if same is None else same + real
                    cross = imag if cross is None else cross + imag
                cross = jnp.where(
                    even, pltpu.roll(cross, SUBLANES - 1, axis=1), pltpu.roll(cross, 1, axis=1)
                )
                results[level][rim + r : rim + r + size, :, i : i + LANES] = same + cross

    def correlate_step(level, low, high):
        for r in range(low, high, SUBLANES):
            for i in tiles:
                field = results[level][rim + r : rim + r + SUBLANES, :, i : i + LANES]
                field = jnp.swapaxes(field, 0, 1)
                part[level, r : r + SUBLANES, i : i + LANES] = field[0] * field[2] + field[1] * field[3]
                part[level, r : r + SUBLANES, half + i : half + i + LANES] = (
                    field[4] * field[6] + field[5] * field[7]
                )

    def groups(low, high):
        found, at = [], low
        while at < high:
            size = 2 if high - at == 4 else min(3, high - at)
            found.append((at, size))
            at += size
        return found

    def sweep(level, degree, spans):
        source, target = levels[level][degree - 1], levels[level][degree]
        for at, size in spans:
            lanes = lax.broadcasted_iota(jnp.int32, (size, SUBLANES, LANES), 2)
            subs = lax.broadcasted_iota(jnp.int32, (size, SUBLANES, LANES), 1)
            sums = []
            inner = []
            for i in tiles:
                field = source[at - 1 : at + size + 1, :, i : i + LANES]
                pair = field[:-1] + field[1:]
                sums.append(pair[:-1] + pair[1:])
                inner.append(field[1:-1])
            for i, total, field in zip(tiles, column_sum(sums, lanes, subs), inner):
                if degree == 1:
                    joint = 0.125 * total
                else:
                    joint = 0.25 * total - paired[at : at + size, :, i : i + LANES]
                if degree < PASSES:
                    paired[at : at + size, :, i : i + LANES] = joint
                value = joint - field
                for edge, absent in ((rim - 1, no_up), (rim + rows, no_down)):
                    if at <= edge < at + size:
                        j = edge - at
                        lines = [value[row : row + 1] for row in range(size)]
                        lines[j] = jnp.where(absent, 0.0, lines[j])
                        value = jnp.concatenate(lines, axis=0)
                target[at : at + size, :, i : i + LANES] = value

    def inside(level):
        for degree in range(1, PASSES):
            if rim + degree < rim + rows - degree:
                sweep(level, degree, groups(rim + degree, rim + rows - degree))

    def outside(level):
        middle = tall // 2
        for degree in range(1, PASSES):
            above = groups(degree, min(rim + degree, middle))
            below = groups(max(rim + rows - degree, middle), tall - degree)
            sweep(level, degree, [span for both in zip(above, below) for span in both])
        sweep(level, PASSES, groups(rim, rim + rows))

    middle = rows // 2
    for level in range(2):
        inside(level)
        if level == 0:
            swap_classes.wait_recv()
        look_up(level)
        if level == 1:
            correlate_step(0, 0, rows)

            @pl.when(step == 1)
            def _():
                swap_image(0, 0).start()
                swap_image(0, 1).start()

        up, down = rims(level)
        pl.when(has_up)(down.wait_recv)
        pl.when(has_down)(up.wait_recv)
        outside(level)
        if level == 0:
            up, down = rims(1)
            weigh(0, 0, rim)
            pl.when(has_up)(up.start)
            weigh(0, rim, rows)
            pl.when(has_down)(down.start)
            zero_rims(1)
        else:
            for piece in range(2):
                weigh(1, piece * middle, (piece + 1) * middle)
                correlate_step(1, piece * middle, (piece + 1) * middle)

                @pl.when(step == 0)
                def _(piece=piece):
                    swap_image(1, piece).start()

    for piece in range(2):
        swap = swap_image(0, piece)
        swap.wait_recv()
        here = pl.ds(piece * middle, middle)
        image_ref[here] = part[step, here] + got[here]
    for piece in range(2):
        swap_image(0, piece).wait_send()
    swap_classes.wait_send()
    for level in range(2):
        up, down = rims(level)
        pl.when(has_up)(up.wait_send)
        pl.when(has_down)(down.wait_send)


def in_kernel(strips, surface, velocity_class, table):
    freqs, parts, rows, full = surface.shape
    half = full // 2
    tall = rows + 2 * PASSES
    f32 = jnp.float32
    fields = pltpu.VMEM((tall, SUBLANES, half), f32)
    return pl.pallas_call(
        functools.partial(migrate, strips),
        out_shape=jax.ShapeDtypeStruct((rows, full), f32),
        in_specs=[pl.BlockSpec(memory_space=pl.ANY)] * 3,
        out_specs=pl.BlockSpec(memory_space=pltpu.VMEM),
        scratch_shapes=[
            pltpu.VMEM((parts, rows, full), f32),
            pltpu.VMEM((2, rows, full), jnp.int32),
            pltpu.SMEM(table.shape, f32),
            pltpu.VMEM((2, PASSES + 1, SUBLANES, LANES), f32),
            pltpu.VMEM((2, PASSES + 1, rows, SUBLANES, half), f32),
            pltpu.VMEM((2, rows, full), f32),
            pltpu.VMEM((rows, full), f32),
        ]
        + [fields] * (PASSES + 3)
        + [
            pltpu.SemaphoreType.DMA((3,)),
            pltpu.SemaphoreType.DMA((2, 2)),
            pltpu.SemaphoreType.DMA((2, 2)),
            pltpu.SemaphoreType.DMA((3,)),
            pltpu.SemaphoreType.DMA((3,)),
        ],
        compiler_params=pltpu.CompilerParams(
            collective_id=0, has_side_effects=True, vmem_limit_bytes=56 * 2**20
        ),
    )(surface, velocity_class.reshape(rows, full), table)[None]


def fits(mesh, surface, velocity_class):
    freqs, parts, rows, full = surface.shape
    return (
        mesh.shape["depth"] == 2
        and velocity_class.shape[0] == 1
        and freqs == 2
        and 2 * parts == SUBLANES
        and rows % (2 * SUBLANES) == 0
        and PASSES <= rows < 2 * PASSES
        and full % (2 * LANES) == 0
        and rows * full <= 2**15
    )


def solution(mesh):
    in_specs = (P(None, None, "strip", None), P("depth", "strip", None), P())
    out_specs = P("depth", "strip", None)

    def part(surface, velocity_class, table):
        if fits(mesh, surface, velocity_class):
            return in_kernel(mesh.shape["strip"], surface, velocity_class, table)
        return body(surface, velocity_class, table)

    return jax.shard_map(part, mesh=mesh, in_specs=in_specs, out_specs=out_specs, check_vma=False)
```

```python
import functools

import jax
import jax.numpy as jnp
from jax import lax
from jax.experimental import pallas as pl
from jax.experimental.pallas import tpu as pltpu
from jax.sharding import PartitionSpec as P

PASSES = 9
CLASSES = 8
LANES = 128
SUBLANES = 8
QUARTERS = 4
MESH = pl.DeviceIdType.MESH


def extended(shard, sides, width):
    for axis, dim in sides:
        devices, length = (lax.axis_size(axis), shard.shape[dim])
        up = [(i, (i + 1) % devices) for i in range(devices - 1)]
        down = [(j, i) for i, j in up]
        last = lax.slice_in_dim(shard, length - width, length, axis=dim)
        initial = lax.slice_in_dim(shard, 0, width, axis=dim)
        before = lax.ppermute(last, axis, up)
        after = lax.ppermute(initial, axis, down)
        shard = jnp.concatenate([before, shard, after], axis=dim)
    return shard


def mcclellan(field):
    lead = [(0, 0)] * (field.ndim - 2)
    padded = jnp.pad(field, lead + [(1, 1), (1, 1)])
    beside = (
        padded[..., 2:, 1:-1]
        + padded[..., :-2, 1:-1]
        + padded[..., 1:-1, 2:]
        + padded[..., 1:-1, :-2]
    )
    corners = (
        padded[..., 2:, 2:] + padded[..., 2:, :-2] + padded[..., :-2, 2:] + padded[..., :-2, :-2]
    )
    return -0.5 * field + 0.25 * beside + 0.125 * corners


def weigh(result, field, real_part, imag_part):
    return jnp.stack(
        [
            result[:, 0] + (real_part * field[:, 0] - imag_part * field[:, 1]),
            result[:, 1] + (real_part * field[:, 1] + imag_part * field[:, 0]),
            result[:, 2] + (real_part * field[:, 2] + imag_part * field[:, 3]),
            result[:, 3] + (real_part * field[:, 3] - imag_part * field[:, 2]),
        ],
        axis=1,
    )


def correlate(fields):
    total = jnp.zeros(fields.shape[2:], jnp.float32)
    for freq_index in range(fields.shape[0]):
        total = total + (
            fields[freq_index, 0] * fields[freq_index, 2]
            + fields[freq_index, 1] * fields[freq_index, 3]
        )
    return total


def tile_halo(sending, rim_width):
    return extended(sending, (("depth", 4), ("strip", 3)), rim_width)


def clip_domain(field, rim_width):
    row_count = field.shape[-2] - 2 * rim_width
    row_ids = (
        lax.axis_index("strip") * row_count
        - rim_width
        + jnp.arange(field.shape[-2], dtype=jnp.int32)
    )
    keep = ((row_ids >= 0) & (row_ids < row_count * lax.axis_size("strip")))[:, None]
    col_count = field.shape[-1] - 2 * rim_width
    col_ids = (
        lax.axis_index("depth") * col_count
        - rim_width
        + jnp.arange(field.shape[-1], dtype=jnp.int32)
    )
    keep = keep & ((col_ids >= 0) & (col_ids < col_count * lax.axis_size("depth")))[None, :]
    return jnp.where(keep, field, 0.0)


def chebyshev(fields, onehot, table_part, rim_width, widen):
    row_count = fields.shape[-2]
    col_count = fields.shape[-1]

    def coefficients(degree):
        pair = jnp.einsum(
            "cij,fcp->fpij", onehot, table_part[:, :, :, degree], precision=lax.Precision.HIGHEST
        )
        return (pair[:, 0], pair[:, 1])

    real_part, imag_part = coefficients(0)
    result = weigh(jnp.zeros_like(fields), fields, real_part, imag_part)
    sending = fields[None]
    widened = widen(sending, rim_width)
    wide_prev = widened[0]
    wide_curr = widened[-1]
    for inner_pass in range(rim_width):
        degree = inner_pass
        if degree == 0:
            following = mcclellan(wide_curr)
        else:
            following = 2.0 * mcclellan(wide_curr) - wide_prev
        following = clip_domain(following, rim_width)
        wide_prev, wide_curr = (wide_curr, following)
        real_part, imag_part = coefficients(degree + 1)
        inner = wide_curr[..., rim_width : rim_width + row_count, :]
        inner = inner[..., rim_width : rim_width + col_count]
        result = weigh(result, inner, real_part, imag_part)
    return result


def body(surface, velocity_class, table):
    classes = jnp.arange(CLASSES, dtype=jnp.int32)
    rim_width = PASSES
    velocity = lax.all_to_all(velocity_class, "depth", split_axis=2, concat_axis=0, tiled=True)
    col_count = velocity.shape[2]
    fields = lax.dynamic_slice_in_dim(surface, lax.axis_index("depth") * col_count, col_count, 3)

    def descend(level_index, state_pair):
        level_fields, image = state_pair
        classes_here = lax.dynamic_index_in_dim(velocity, level_index, 0, keepdims=False)
        onehot = (classes_here[None] == classes[:, None, None]).astype(jnp.float32)
        level_fields = chebyshev(level_fields, onehot, table, rim_width, tile_halo)
        image = lax.dynamic_update_index_in_dim(image, correlate(level_fields), level_index, 0)
        return (level_fields, image)

    initial = (fields, jnp.zeros((velocity.shape[0], velocity.shape[1], col_count), jnp.float32))
    fields, image = lax.fori_loop(0, velocity.shape[0], descend, initial)
    return lax.all_to_all(image, "depth", split_axis=0, concat_axis=2, tiled=True)


def column_sum(tiles, lane, sub):
    rights = [pltpu.roll(t, 1, axis=2) for t in tiles]
    lefts = [pltpu.roll(t, LANES - 1, axis=2) for t in tiles]
    before = jnp.where(sub < 2, 0.0, pltpu.roll(rights[-1], 2, axis=1))
    after = jnp.where(sub < SUBLANES - 2, pltpu.roll(lefts[0], SUBLANES - 2, axis=1), 0.0)
    sums = []
    for i, t in enumerate(tiles):
        right = jnp.where(lane == 0, rights[i - 1] if i else before, rights[i])
        left = jnp.where(lane == LANES - 1, lefts[i + 1] if i + 1 < len(tiles) else after, lefts[i])
        sums.append((right + left) + (t + t))
    return sums


def migrate(strips, surface_ref, velocity_ref, table_ref, image_ref, *scratch):
    raw, classes, numbers, coef, spot, part, got = scratch[:7]
    per_group = PASSES + 3
    held = [scratch[7 + g * per_group : 7 + (g + 1) * per_group] for g in range(2)]
    load_sem, rim_send, rim_recv, swap_send, swap_recv = scratch[7 + 2 * per_group :]
    first = [h[0] for h in held]
    second = [h[1] for h in held]
    paired = [h[2] for h in held]
    terms = [[[first, second][level][g]] + list(held[g][3:]) for g in range(2) for level in range(2)]

    def term(g, level):
        return terms[2 * g + level]

    rows, full = velocity_ref.shape
    wide = full // QUARTERS
    rim = PASSES
    tall = rows + 2 * rim
    step = lax.axis_index("depth")
    strip = lax.axis_index("strip")
    other = 1 - step
    has_up = strip > 0
    has_down = strip < strips - 1
    no_up = jnp.logical_not(has_up)
    no_down = jnp.logical_not(has_down)
    lane = lax.broadcasted_iota(jnp.int32, (SUBLANES, LANES), 1)
    sub = lax.broadcasted_iota(jnp.int32, (SUBLANES, LANES), 0)
    tiles = range(0, wide, LANES)

    load_surface = pltpu.make_async_copy(surface_ref.at[step], raw, load_sem.at[0])
    load_classes = pltpu.make_async_copy(velocity_ref, classes.at[step], load_sem.at[1])
    load_table = pltpu.make_async_copy(table_ref, numbers, load_sem.at[2])
    load_surface.start()
    load_classes.start()
    load_table.start()

    barrier = pltpu.get_barrier_semaphore()
    pl.semaphore_signal(barrier, inc=1, device_id={"depth": other}, device_id_type=MESH)

    @pl.when(has_up)
    def _():
        pl.semaphore_signal(barrier, inc=1, device_id={"strip": strip - 1}, device_id_type=MESH)

    @pl.when(has_down)
    def _():
        pl.semaphore_signal(barrier, inc=1, device_id={"strip": strip + 1}, device_id_type=MESH)

    load_surface.wait()
    for g in range(2):
        for r in range(0, rows, SUBLANES):
            for i in tiles:
                block = jnp.concatenate(
                    [
                        raw[2 * g : 2 * g + 2, r : r + SUBLANES, q * wide + i : q * wide + i + LANES]
                        for q in range(QUARTERS)
                    ],
                    axis=0,
                )
                first[g][rim + r : rim + r + SUBLANES, :, i : i + LANES] = jnp.swapaxes(block, 0, 1)

    load_classes.wait()
    pl.semaphore_wait(barrier, 1 + has_up.astype(jnp.int32) + has_down.astype(jnp.int32))

    def rims(g, level):
        base = term(g, level)[0]
        up = pltpu.make_async_remote_copy(
            src_ref=base.at[pl.ds(rim, rim)],
            dst_ref=base.at[pl.ds(rim + rows, rim)],
            send_sem=rim_send.at[g, level, 0],
            recv_sem=rim_recv.at[g, level, 0],
            device_id={"strip": strip - 1},
            device_id_type=MESH,
        )
        down = pltpu.make_async_remote_copy(
            src_ref=base.at[pl.ds(rows, rim)],
            dst_ref=base.at[pl.ds(0, rim)],
            send_sem=rim_send.at[g, level, 1],
            recv_sem=rim_recv.at[g, level, 1],
            device_id={"strip": strip + 1},
            device_id_type=MESH,
        )
        return up, down

    def await_rims(g, level):
        up, down = rims(g, level)
        pl.when(has_up)(down.wait_recv)
        pl.when(has_down)(up.wait_recv)

    def zero_rims(level):
        @pl.when(no_up)
        def _():
            for g in range(2):
                term(g, level)[0][:rim] = jnp.zeros((rim, SUBLANES, wide), jnp.float32)

        @pl.when(no_down)
        def _():
            for g in range(2):
                term(g, level)[0][rim + rows :] = jnp.zeros((rim, SUBLANES, wide), jnp.float32)

    def swap_image(level, piece):
        here = pl.ds(piece * (rows // 2), rows // 2)
        return pltpu.make_async_remote_copy(
            src_ref=part.at[level, here],
            dst_ref=got.at[here],
            send_sem=swap_send.at[1 + piece],
            recv_sem=swap_recv.at[1 + piece],
            device_id={"depth": other},
            device_id_type=MESH,
        )

    for g in range(2):
        up, down = rims(g, 0)
        pl.when(has_up)(up.start)
        pl.when(has_down)(down.start)
    swap_classes = pltpu.make_async_remote_copy(
        src_ref=classes.at[step],
        dst_ref=classes.at[step],
        send_sem=swap_send.at[0],
        recv_sem=swap_recv.at[0],
        device_id={"depth": other},
        device_id_type=MESH,
    )
    swap_classes.start()
    zero_rims(0)
    zero_rims(1)

    sign = jnp.where(lax.rem(sub, 2) == 1, -1.0, 1.0)
    load_table.wait()

    def fill(degree, carry):
        for p in range(2):
            spread = jnp.zeros((SUBLANES, LANES), jnp.float32)
            for c in range(CLASSES):
                spread = jnp.where(lane == c, numbers[step, c, p, degree], spread)
            coef[p, degree] = spread * sign if p else spread
        return carry

    lax.fori_loop(0, PASSES + 1, fill, 0)

    def look_up(level):
        def block(b, carry):
            for j in range(4):
                r = b * 4 + j
                kind = classes[level, pl.ds(r, 1), :]
                for i in tiles:
                    index = None
                    for q in range(QUARTERS):
                        at = q * wide + i
                        spread = jnp.broadcast_to(kind[:, at : at + LANES], (SUBLANES, LANES))
                        index = spread if q == 0 else jnp.where(sub < 2 * q, index, spread)
                    for p in range(2):
                        for k in range(PASSES + 1):
                            spot[p, k, r, :, i : i + LANES] = jnp.take_along_axis(
                                coef[p, k], index, axis=1, mode="promise_in_bounds"
                            )
            return carry

        lax.fori_loop(0, rows // 4, block, 0)

    results = (second, paired)

    def weigh(g, level, low, high):
        series = term(g, level)
        for r in range(low, high, 4):
            size = min(4, high - r)
            even = lax.rem(lax.broadcasted_iota(jnp.int32, (size, SUBLANES, LANES), 1), 2) == 0
            for i in tiles:
                same = cross = None
                for k in range(PASSES + 1):
                    field = series[k][rim + r : rim + r + size, :, i : i + LANES]
                    real = spot[0, k, r : r + size, :, i : i + LANES] * field
                    imag = spot[1, k, r : r + size, :, i : i + LANES] * field
                    same = real if same is None else same + real
                    cross = imag if cross is None else cross + imag
                cross = jnp.where(
                    even, pltpu.roll(cross, SUBLANES - 1, axis=1), pltpu.roll(cross, 1, axis=1)
                )
                results[level][g][rim + r : rim + r + size, :, i : i + LANES] = (
                    same - cross if g else same + cross
                )

    def correlate_step(level, low, high):
        for r in range(low, high, SUBLANES):
            for i in tiles:
                source, receiver = (
                    results[level][g][rim + r : rim + r + SUBLANES, :, i : i + LANES] for g in range(2)
                )
                product = jnp.swapaxes(source * receiver, 0, 1)
                for q in range(QUARTERS):
                    part[level, r : r + SUBLANES, q * wide + i : q * wide + i + LANES] = (
                        product[2 * q] + product[2 * q + 1]
                    )

    def groups(low, high):
        count = max(1, -(-(high - low) // 5))
        found, at = [], low
        for n in range(count):
            size = (high - at) // (count - n)
            found.append((at, size))
            at += size
        return found

    def sweep(g, level, degree, spans):
        source, target = term(g, level)[degree - 1], term(g, level)[degree]
        for at, size in spans:
            lanes = lax.broadcasted_iota(jnp.int32, (size, SUBLANES, LANES), 2)
            subs = lax.broadcasted_iota(jnp.int32, (size, SUBLANES, LANES), 1)
            sums = []
            inner = []
            for i in tiles:
                field = source[at - 1 : at + size + 1, :, i : i + LANES]
                pair = field[:-1] + field[1:]
                sums.append(pair[:-1] + pair[1:])
                inner.append(field[1:-1])
            for i, total, field in zip(tiles, column_sum(sums, lanes, subs), inner):
                if degree == 1:
                    joint = 0.125 * total
                else:
                    joint = 0.25 * total - paired[g][at : at + size, :, i : i + LANES]
                if degree < PASSES:
                    paired[g][at : at + size, :, i : i + LANES] = joint
                value = joint - field
                for edge, absent in ((rim - 1, no_up), (rim + rows, no_down)):
                    if at <= edge < at + size:
                        lines = [value[row : row + 1] for row in range(size)]
                        lines[edge - at] = jnp.where(absent, 0.0, lines[edge - at])
                        value = jnp.concatenate(lines, axis=0)
                target[at : at + size, :, i : i + LANES] = value

    def inside(g, level, degree):
        low, high = rim + degree, rim + rows - degree
        if degree < PASSES and low < high:
            sweep(g, level, degree, groups(low, high))

    def outside(g, level, degree):
        if degree == PASSES:
            return sweep(g, level, degree, groups(rim, rim + rows))
        middle = tall // 2
        above = groups(degree, min(rim + degree, middle))
        below = groups(max(rim + rows - degree, middle), tall - degree)
        sweep(g, level, degree, [span for both in zip(above, below) for span in both])

    degrees = range(1, PASSES + 1)
    for degree in degrees:
        inside(0, 0, degree)
        inside(1, 0, degree)
    swap_classes.wait_recv()
    look_up(0)
    for g in range(2):
        await_rims(g, 0)
        for degree in degrees:
            outside(g, 0, degree)
            if g == 1:
                inside(0, 1, degree)
        up, down = rims(g, 1)
        weigh(g, 0, 0, rim)
        pl.when(has_up)(up.start)
        weigh(g, 0, rim, rows)
        pl.when(has_down)(down.start)

    look_up(1)
    correlate_step(0, 0, rows)

    @pl.when(step == 1)
    def _():
        swap_image(0, 0).start()
        swap_image(0, 1).start()

    await_rims(0, 1)
    for degree in degrees:
        outside(0, 1, degree)
        inside(1, 1, degree)
    weigh(0, 1, 0, rows)
    await_rims(1, 1)
    for degree in degrees:
        outside(1, 1, degree)
    half = rows // 2
    for piece in range(2):
        weigh(1, 1, piece * half, (piece + 1) * half)
        correlate_step(1, piece * half, (piece + 1) * half)

        @pl.when(step == 0)
        def _(piece=piece):
            swap_image(1, piece).start()

    for piece in range(2):
        swap_image(0, piece).wait_recv()
        here = pl.ds(piece * half, half)
        image_ref[here] = part[step, here] + got[here]
    for piece in range(2):
        swap_image(0, piece).wait_send()
    swap_classes.wait_send()
    for g in range(2):
        for level in range(2):
            up, down = rims(g, level)
            pl.when(has_up)(up.wait_send)
            pl.when(has_down)(down.wait_send)


def in_kernel(strips, surface, velocity_class, table):
    freqs, parts, rows, full = surface.shape
    wide = full // QUARTERS
    tall = rows + 2 * PASSES
    f32 = jnp.float32
    fields = pltpu.VMEM((tall, SUBLANES, wide), f32)
    return pl.pallas_call(
        functools.partial(migrate, strips),
        out_shape=jax.ShapeDtypeStruct((rows, full), f32),
        in_specs=[pl.BlockSpec(memory_space=pl.ANY)] * 3,
        out_specs=pl.BlockSpec(memory_space=pltpu.VMEM),
        scratch_shapes=[
            pltpu.VMEM((parts, rows, full), f32),
            pltpu.VMEM((2, rows, full), jnp.int32),
            pltpu.SMEM(table.shape, f32),
            pltpu.VMEM((2, PASSES + 1, SUBLANES, LANES), f32),
            pltpu.VMEM((2, PASSES + 1, rows, SUBLANES, wide), f32),
            pltpu.VMEM((2, rows, full), f32),
            pltpu.VMEM((rows, full), f32),
        ]
        + [fields] * (2 * (PASSES + 3))
        + [
            pltpu.SemaphoreType.DMA((3,)),
            pltpu.SemaphoreType.DMA((2, 2, 2)),
            pltpu.SemaphoreType.DMA((2, 2, 2)),
            pltpu.SemaphoreType.DMA((3,)),
            pltpu.SemaphoreType.DMA((3,)),
        ],
        compiler_params=pltpu.CompilerParams(
            collective_id=0, has_side_effects=True, vmem_limit_bytes=56 * 2**20
        ),
    )(surface, velocity_class.reshape(rows, full), table)[None]


def fits(mesh, surface, velocity_class):
    freqs, parts, rows, full = surface.shape
    return (
        mesh.shape["depth"] == 2
        and velocity_class.shape[0] == 1
        and freqs == 2
        and parts == 4
        and rows % (2 * SUBLANES) == 0
        and PASSES <= rows < 2 * PASSES
        and full % (QUARTERS * LANES) == 0
        and rows * full <= 2**15
    )


def solution(mesh):
    in_specs = (P(None, None, "strip", None), P("depth", "strip", None), P())
    out_specs = P("depth", "strip", None)

    def part(surface, velocity_class, table):
        if fits(mesh, surface, velocity_class):
            return in_kernel(mesh.shape["strip"], surface, velocity_class, table)
        return body(surface, velocity_class, table)

    return jax.shard_map(part, mesh=mesh, in_specs=in_specs, out_specs=out_specs, check_vma=False)
```

```python
import functools

import jax
import jax.numpy as jnp
from jax import lax
from jax.experimental import pallas as pl
from jax.experimental.pallas import tpu as pltpu
from jax.sharding import PartitionSpec as P

PASSES = 9
CLASSES = 8
LANES = 128
SUBLANES = 8
QUARTERS = 4
MESH = pl.DeviceIdType.MESH


def extended(shard, sides, width):
    for axis, dim in sides:
        devices, length = (lax.axis_size(axis), shard.shape[dim])
        up = [(i, (i + 1) % devices) for i in range(devices - 1)]
        down = [(j, i) for i, j in up]
        last = lax.slice_in_dim(shard, length - width, length, axis=dim)
        initial = lax.slice_in_dim(shard, 0, width, axis=dim)
        before = lax.ppermute(last, axis, up)
        after = lax.ppermute(initial, axis, down)
        shard = jnp.concatenate([before, shard, after], axis=dim)
    return shard


def mcclellan(field):
    lead = [(0, 0)] * (field.ndim - 2)
    padded = jnp.pad(field, lead + [(1, 1), (1, 1)])
    beside = (
        padded[..., 2:, 1:-1]
        + padded[..., :-2, 1:-1]
        + padded[..., 1:-1, 2:]
        + padded[..., 1:-1, :-2]
    )
    corners = (
        padded[..., 2:, 2:] + padded[..., 2:, :-2] + padded[..., :-2, 2:] + padded[..., :-2, :-2]
    )
    return -0.5 * field + 0.25 * beside + 0.125 * corners


def weigh(result, field, real_part, imag_part):
    return jnp.stack(
        [
            result[:, 0] + (real_part * field[:, 0] - imag_part * field[:, 1]),
            result[:, 1] + (real_part * field[:, 1] + imag_part * field[:, 0]),
            result[:, 2] + (real_part * field[:, 2] + imag_part * field[:, 3]),
            result[:, 3] + (real_part * field[:, 3] - imag_part * field[:, 2]),
        ],
        axis=1,
    )


def correlate(fields):
    total = jnp.zeros(fields.shape[2:], jnp.float32)
    for freq_index in range(fields.shape[0]):
        total = total + (
            fields[freq_index, 0] * fields[freq_index, 2]
            + fields[freq_index, 1] * fields[freq_index, 3]
        )
    return total


def tile_halo(sending, rim_width):
    return extended(sending, (("depth", 4), ("strip", 3)), rim_width)


def clip_domain(field, rim_width):
    row_count = field.shape[-2] - 2 * rim_width
    row_ids = (
        lax.axis_index("strip") * row_count
        - rim_width
        + jnp.arange(field.shape[-2], dtype=jnp.int32)
    )
    keep = ((row_ids >= 0) & (row_ids < row_count * lax.axis_size("strip")))[:, None]
    col_count = field.shape[-1] - 2 * rim_width
    col_ids = (
        lax.axis_index("depth") * col_count
        - rim_width
        + jnp.arange(field.shape[-1], dtype=jnp.int32)
    )
    keep = keep & ((col_ids >= 0) & (col_ids < col_count * lax.axis_size("depth")))[None, :]
    return jnp.where(keep, field, 0.0)


def chebyshev(fields, onehot, table_part, rim_width, widen):
    row_count = fields.shape[-2]
    col_count = fields.shape[-1]

    def coefficients(degree):
        pair = jnp.einsum(
            "cij,fcp->fpij", onehot, table_part[:, :, :, degree], precision=lax.Precision.HIGHEST
        )
        return (pair[:, 0], pair[:, 1])

    real_part, imag_part = coefficients(0)
    result = weigh(jnp.zeros_like(fields), fields, real_part, imag_part)
    sending = fields[None]
    widened = widen(sending, rim_width)
    wide_prev = widened[0]
    wide_curr = widened[-1]
    for inner_pass in range(rim_width):
        degree = inner_pass
        if degree == 0:
            following = mcclellan(wide_curr)
        else:
            following = 2.0 * mcclellan(wide_curr) - wide_prev
        following = clip_domain(following, rim_width)
        wide_prev, wide_curr = (wide_curr, following)
        real_part, imag_part = coefficients(degree + 1)
        inner = wide_curr[..., rim_width : rim_width + row_count, :]
        inner = inner[..., rim_width : rim_width + col_count]
        result = weigh(result, inner, real_part, imag_part)
    return result


def body(surface, velocity_class, table):
    classes = jnp.arange(CLASSES, dtype=jnp.int32)
    rim_width = PASSES
    velocity = lax.all_to_all(velocity_class, "depth", split_axis=2, concat_axis=0, tiled=True)
    col_count = velocity.shape[2]
    fields = lax.dynamic_slice_in_dim(surface, lax.axis_index("depth") * col_count, col_count, 3)

    def descend(level_index, state_pair):
        level_fields, image = state_pair
        classes_here = lax.dynamic_index_in_dim(velocity, level_index, 0, keepdims=False)
        onehot = (classes_here[None] == classes[:, None, None]).astype(jnp.float32)
        level_fields = chebyshev(level_fields, onehot, table, rim_width, tile_halo)
        image = lax.dynamic_update_index_in_dim(image, correlate(level_fields), level_index, 0)
        return (level_fields, image)

    initial = (fields, jnp.zeros((velocity.shape[0], velocity.shape[1], col_count), jnp.float32))
    fields, image = lax.fori_loop(0, velocity.shape[0], descend, initial)
    return lax.all_to_all(image, "depth", split_axis=0, concat_axis=2, tiled=True)


def pick(block, index):
    return jnp.take_along_axis(block, index, axis=1, mode="promise_in_bounds")


def interleaved(blocks):
    count = len(blocks)
    lane = lax.broadcasted_iota(jnp.int32, (SUBLANES, LANES), 1)
    found = []
    for j in range(count):
        index = lax.rem(lane * count + j, LANES)
        tile = pick(blocks[0], index)
        for n in range(1, count):
            tile = jnp.where(lane * count >= n * LANES, pick(blocks[n], index), tile)
        found.append(tile)
    return found


def restored(blocks):
    count = len(blocks)
    lane = lax.broadcasted_iota(jnp.int32, (SUBLANES, LANES), 1)
    found = []
    for n in range(count):
        index = (lane + n * LANES) // count
        tile = pick(blocks[0], index)
        for j in range(1, count):
            tile = jnp.where(lax.rem(lane, count) == j, pick(blocks[j], index), tile)
        found.append(tile)
    return found


def column_sum(tiles, lane, sub):
    right = pltpu.roll(tiles[-1], 1, axis=2)
    left = pltpu.roll(tiles[0], LANES - 1, axis=2)
    before = jnp.where(sub < 2, 0.0, pltpu.roll(right, 2, axis=1))
    after = jnp.where(sub < SUBLANES - 2, pltpu.roll(left, SUBLANES - 2, axis=1), 0.0)
    line = [jnp.where(lane == 0, before, right)] + tiles + [jnp.where(lane == LANES - 1, after, left)]
    pairs = [p + q for p, q in zip(line[:-1], line[1:])]
    return [p + q for p, q in zip(pairs[:-1], pairs[1:])]


def migrate(strips, surface_ref, velocity_ref, table_ref, image_ref, *scratch):
    raw, classes, numbers, coef, spot, part, got, mixed = scratch[:8]
    per_group = PASSES + 3
    held = [scratch[8 + g * per_group : 8 + (g + 1) * per_group] for g in range(2)]
    load_sem, rim_send, rim_recv, swap_send, swap_recv = scratch[8 + 2 * per_group :]
    first = [h[0] for h in held]
    second = [h[1] for h in held]
    paired = [h[2] for h in held]
    terms = [[[first, second][level][g]] + list(held[g][3:]) for g in range(2) for level in range(2)]

    def term(g, level):
        return terms[2 * g + level]

    rows, full = velocity_ref.shape
    wide = full // QUARTERS
    rim = PASSES
    tall = rows + 2 * rim
    step = lax.axis_index("depth")
    strip = lax.axis_index("strip")
    other = 1 - step
    has_up = strip > 0
    has_down = strip < strips - 1
    no_up = jnp.logical_not(has_up)
    no_down = jnp.logical_not(has_down)
    lane = lax.broadcasted_iota(jnp.int32, (SUBLANES, LANES), 1)
    sub = lax.broadcasted_iota(jnp.int32, (SUBLANES, LANES), 0)
    tiles = range(0, wide, LANES)

    load_surface = pltpu.make_async_copy(surface_ref.at[step], raw, load_sem.at[0])
    load_classes = pltpu.make_async_copy(velocity_ref, classes.at[step], load_sem.at[1])
    load_table = pltpu.make_async_copy(table_ref, numbers, load_sem.at[2])
    load_surface.start()
    load_classes.start()
    load_table.start()

    barrier = pltpu.get_barrier_semaphore()
    pl.semaphore_signal(barrier, inc=1, device_id={"depth": other}, device_id_type=MESH)

    @pl.when(has_up)
    def _():
        pl.semaphore_signal(barrier, inc=1, device_id={"strip": strip - 1}, device_id_type=MESH)

    @pl.when(has_down)
    def _():
        pl.semaphore_signal(barrier, inc=1, device_id={"strip": strip + 1}, device_id_type=MESH)

    load_surface.wait()
    for g in range(2):
        for r in range(0, rows, SUBLANES):
            parts = [
                interleaved(
                    [
                        raw[2 * g + c, r : r + SUBLANES, q * wide + i : q * wide + i + LANES]
                        for i in tiles
                    ]
                )
                for q in range(QUARTERS)
                for c in range(2)
            ]
            for j, i in enumerate(tiles):
                block = jnp.stack([part_tiles[j] for part_tiles in parts])
                first[g][rim + r : rim + r + SUBLANES, :, i : i + LANES] = jnp.swapaxes(block, 0, 1)

    load_classes.wait()
    pl.semaphore_wait(barrier, 1 + has_up.astype(jnp.int32) + has_down.astype(jnp.int32))

    def rims(g, level):
        base = term(g, level)[0]
        up = pltpu.make_async_remote_copy(
            src_ref=base.at[pl.ds(rim, rim)],
            dst_ref=base.at[pl.ds(rim + rows, rim)],
            send_sem=rim_send.at[g, level, 0],
            recv_sem=rim_recv.at[g, level, 0],
            device_id={"strip": strip - 1},
            device_id_type=MESH,
        )
        down = pltpu.make_async_remote_copy(
            src_ref=base.at[pl.ds(rows, rim)],
            dst_ref=base.at[pl.ds(0, rim)],
            send_sem=rim_send.at[g, level, 1],
            recv_sem=rim_recv.at[g, level, 1],
            device_id={"strip": strip + 1},
            device_id_type=MESH,
        )
        return up, down

    def await_rims(g, level):
        up, down = rims(g, level)
        pl.when(has_up)(down.wait_recv)
        pl.when(has_down)(up.wait_recv)

    def zero_rims(level):
        @pl.when(no_up)
        def _():
            for g in range(2):
                term(g, level)[0][:rim] = jnp.zeros((rim, SUBLANES, wide), jnp.float32)

        @pl.when(no_down)
        def _():
            for g in range(2):
                term(g, level)[0][rim + rows :] = jnp.zeros((rim, SUBLANES, wide), jnp.float32)

    def swap_image(level, piece):
        here = pl.ds(piece * (rows // 2), rows // 2)
        return pltpu.make_async_remote_copy(
            src_ref=part.at[level, here],
            dst_ref=got.at[here],
            send_sem=swap_send.at[1 + piece],
            recv_sem=swap_recv.at[1 + piece],
            device_id={"depth": other},
            device_id_type=MESH,
        )

    for g in range(2):
        up, down = rims(g, 0)
        pl.when(has_up)(up.start)
        pl.when(has_down)(down.start)
    swap_classes = pltpu.make_async_remote_copy(
        src_ref=classes.at[step],
        dst_ref=classes.at[step],
        send_sem=swap_send.at[0],
        recv_sem=swap_recv.at[0],
        device_id={"depth": other},
        device_id_type=MESH,
    )
    swap_classes.start()
    zero_rims(0)
    zero_rims(1)

    sign = jnp.where(lax.rem(sub, 2) == 1, -1.0, 1.0)
    load_table.wait()

    def fill(degree, carry):
        for p in range(2):
            spread = jnp.zeros((SUBLANES, LANES), jnp.float32)
            for c in range(CLASSES):
                spread = jnp.where(lane == c, numbers[step, c, p, degree], spread)
            coef[p, degree] = spread * sign if p else spread
        return carry

    lax.fori_loop(0, PASSES + 1, fill, 0)

    def look_up(level):
        for r in range(0, rows, SUBLANES):
            for q in range(QUARTERS):
                found = interleaved(
                    [
                        classes[level, r : r + SUBLANES, q * wide + i : q * wide + i + LANES]
                        for i in tiles
                    ]
                )
                for i, tile in zip(tiles, found):
                    mixed[r : r + SUBLANES, q * wide + i : q * wide + i + LANES] = tile

        def block(b, carry):
            for j in range(4):
                r = b * 4 + j
                kind = mixed[pl.ds(r, 1), :]
                for i in tiles:
                    index = None
                    for q in range(QUARTERS):
                        at = q * wide + i
                        spread = jnp.broadcast_to(kind[:, at : at + LANES], (SUBLANES, LANES))
                        index = spread if q == 0 else jnp.where(sub < 2 * q, index, spread)
                    for p in range(2):
                        for k in range(PASSES + 1):
                            spot[p, k, r, :, i : i + LANES] = jnp.take_along_axis(
                                coef[p, k], index, axis=1, mode="promise_in_bounds"
                            )
            return carry

        lax.fori_loop(0, rows // 4, block, 0)

    results = (second, paired)

    def weigh(g, level, low, high):
        series = term(g, level)
        for r in range(low, high, 4):
            size = min(4, high - r)
            even = lax.rem(lax.broadcasted_iota(jnp.int32, (size, SUBLANES, LANES), 1), 2) == 0
            for i in tiles:
                same = cross = None
                for k in range(PASSES + 1):
                    field = series[k][rim + r : rim + r + size, :, i : i + LANES]
                    real = spot[0, k, r : r + size, :, i : i + LANES] * field
                    imag = spot[1, k, r : r + size, :, i : i + LANES] * field
                    same = real if same is None else same + real
                    cross = imag if cross is None else cross + imag
                cross = jnp.where(
                    even, pltpu.roll(cross, SUBLANES - 1, axis=1), pltpu.roll(cross, 1, axis=1)
                )
                results[level][g][rim + r : rim + r + size, :, i : i + LANES] = (
                    same - cross if g else same + cross
                )

    def correlate_step(level, low, high):
        for r in range(low, high, SUBLANES):
            for i in tiles:
                source, receiver = (
                    results[level][g][rim + r : rim + r + SUBLANES, :, i : i + LANES] for g in range(2)
                )
                product = jnp.swapaxes(source * receiver, 0, 1)
                for q in range(QUARTERS):
                    part[level, r : r + SUBLANES, q * wide + i : q * wide + i + LANES] = (
                        product[2 * q] + product[2 * q + 1]
                    )

    def groups(low, high):
        count = max(1, -(-(high - low) // 5))
        found, at = [], low
        for n in range(count):
            size = (high - at) // (count - n)
            found.append((at, size))
            at += size
        return found

    def sweep(g, level, degree, spans):
        source, target = term(g, level)[degree - 1], term(g, level)[degree]
        for at, size in spans:
            lanes = lax.broadcasted_iota(jnp.int32, (size, SUBLANES, LANES), 2)
            subs = lax.broadcasted_iota(jnp.int32, (size, SUBLANES, LANES), 1)
            sums = []
            inner = []
            for i in tiles:
                field = source[at - 1 : at + size + 1, :, i : i + LANES]
                pair = field[:-1] + field[1:]
                sums.append(pair[:-1] + pair[1:])
                inner.append(field[1:-1])
            for i, total, field in zip(tiles, column_sum(sums, lanes, subs), inner):
                if degree == 1:
                    joint = 0.125 * total
                else:
                    joint = 0.25 * total - paired[g][at : at + size, :, i : i + LANES]
                if degree < PASSES:
                    paired[g][at : at + size, :, i : i + LANES] = joint
                value = joint - field
                for edge, absent in ((rim - 1, no_up), (rim + rows, no_down)):
                    if at <= edge < at + size:
                        lines = [value[row : row + 1] for row in range(size)]
                        lines[edge - at] = jnp.where(absent, 0.0, lines[edge - at])
                        value = jnp.concatenate(lines, axis=0)
                target[at : at + size, :, i : i + LANES] = value

    def inside(g, level, degree):
        low, high = rim + degree, rim + rows - degree
        if degree < PASSES and low < high:
            sweep(g, level, degree, groups(low, high))

    def outside(g, level, degree):
        if degree == PASSES:
            return sweep(g, level, degree, groups(rim, rim + rows))
        middle = tall // 2
        above = groups(degree, min(rim + degree, middle))
        below = groups(max(rim + rows - degree, middle), tall - degree)
        sweep(g, level, degree, [span for both in zip(above, below) for span in both])

    degrees = range(1, PASSES + 1)
    for degree in degrees:
        inside(0, 0, degree)
        inside(1, 0, degree)
    swap_classes.wait_recv()
    look_up(0)
    for g in range(2):
        await_rims(g, 0)
        for degree in degrees:
            outside(g, 0, degree)
            if g == 1:
                inside(0, 1, degree)
        up, down = rims(g, 1)
        weigh(g, 0, 0, rim)
        pl.when(has_up)(up.start)
        weigh(g, 0, rim, rows)
        pl.when(has_down)(down.start)

    look_up(1)
    correlate_step(0, 0, rows)

    @pl.when(step == 1)
    def _():
        swap_image(0, 0).start()
        swap_image(0, 1).start()

    await_rims(0, 1)
    for degree in degrees:
        outside(0, 1, degree)
        inside(1, 1, degree)
    weigh(0, 1, 0, rows)
    await_rims(1, 1)
    for degree in degrees:
        outside(1, 1, degree)
    half = rows // 2
    for piece in range(2):
        weigh(1, 1, piece * half, (piece + 1) * half)
        correlate_step(1, piece * half, (piece + 1) * half)

        @pl.when(step == 0)
        def _(piece=piece):
            swap_image(1, piece).start()

    for piece in range(2):
        swap_image(0, piece).wait_recv()
        for r in range(piece * half, (piece + 1) * half, SUBLANES):
            here = slice(r, r + SUBLANES)
            for q in range(QUARTERS):
                places = [slice(q * wide + i, q * wide + i + LANES) for i in tiles]
                found = restored([part[step, here, place] + got[here, place] for place in places])
                for place, tile in zip(places, found):
                    image_ref[here, place] = tile
    for piece in range(2):
        swap_image(0, piece).wait_send()
    swap_classes.wait_send()
    for g in range(2):
        for level in range(2):
            up, down = rims(g, level)
            pl.when(has_up)(up.wait_send)
            pl.when(has_down)(down.wait_send)


def in_kernel(strips, surface, velocity_class, table):
    freqs, parts, rows, full = surface.shape
    wide = full // QUARTERS
    tall = rows + 2 * PASSES
    f32 = jnp.float32
    fields = pltpu.VMEM((tall, SUBLANES, wide), f32)
    return pl.pallas_call(
        functools.partial(migrate, strips),
        out_shape=jax.ShapeDtypeStruct((rows, full), f32),
        in_specs=[pl.BlockSpec(memory_space=pl.ANY)] * 3,
        out_specs=pl.BlockSpec(memory_space=pltpu.VMEM),
        scratch_shapes=[
            pltpu.VMEM((parts, rows, full), f32),
            pltpu.VMEM((2, rows, full), jnp.int32),
            pltpu.SMEM(table.shape, f32),
            pltpu.VMEM((2, PASSES + 1, SUBLANES, LANES), f32),
            pltpu.VMEM((2, PASSES + 1, rows, SUBLANES, wide), f32),
            pltpu.VMEM((2, rows, full), f32),
            pltpu.VMEM((rows, full), f32),
            pltpu.VMEM((rows, full), jnp.int32),
        ]
        + [fields] * (2 * (PASSES + 3))
        + [
            pltpu.SemaphoreType.DMA((3,)),
            pltpu.SemaphoreType.DMA((2, 2, 2)),
            pltpu.SemaphoreType.DMA((2, 2, 2)),
            pltpu.SemaphoreType.DMA((3,)),
            pltpu.SemaphoreType.DMA((3,)),
        ],
        compiler_params=pltpu.CompilerParams(
            collective_id=0, has_side_effects=True, vmem_limit_bytes=56 * 2**20
        ),
    )(surface, velocity_class.reshape(rows, full), table)[None]


def fits(mesh, surface, velocity_class):
    freqs, parts, rows, full = surface.shape
    return (
        mesh.shape["depth"] == 2
        and velocity_class.shape[0] == 1
        and freqs == 2
        and parts == 4
        and rows % (2 * SUBLANES) == 0
        and PASSES <= rows < 2 * PASSES
        and full % (QUARTERS * LANES) == 0
        and LANES % (full // (QUARTERS * LANES)) == 0
        and rows * full <= 2**15
    )


def solution(mesh):
    in_specs = (P(None, None, "strip", None), P("depth", "strip", None), P())
    out_specs = P("depth", "strip", None)

    def part(surface, velocity_class, table):
        if fits(mesh, surface, velocity_class):
            return in_kernel(mesh.shape["strip"], surface, velocity_class, table)
        return body(surface, velocity_class, table)

    return jax.shard_map(part, mesh=mesh, in_specs=in_specs, out_specs=out_specs, check_vma=False)
```

```python
import functools

import jax
import jax.numpy as jnp
from jax import lax
from jax.experimental import pallas as pl
from jax.experimental.pallas import tpu as pltpu
from jax.sharding import PartitionSpec as P

PASSES = 9
CLASSES = 8
LANES = 128
SUBLANES = 8
QUARTERS = 4
MESH = pl.DeviceIdType.MESH


def extended(shard, sides, width):
    for axis, dim in sides:
        devices, length = (lax.axis_size(axis), shard.shape[dim])
        up = [(i, (i + 1) % devices) for i in range(devices - 1)]
        down = [(j, i) for i, j in up]
        last = lax.slice_in_dim(shard, length - width, length, axis=dim)
        initial = lax.slice_in_dim(shard, 0, width, axis=dim)
        before = lax.ppermute(last, axis, up)
        after = lax.ppermute(initial, axis, down)
        shard = jnp.concatenate([before, shard, after], axis=dim)
    return shard


def mcclellan(field):
    lead = [(0, 0)] * (field.ndim - 2)
    padded = jnp.pad(field, lead + [(1, 1), (1, 1)])
    beside = (
        padded[..., 2:, 1:-1]
        + padded[..., :-2, 1:-1]
        + padded[..., 1:-1, 2:]
        + padded[..., 1:-1, :-2]
    )
    corners = (
        padded[..., 2:, 2:] + padded[..., 2:, :-2] + padded[..., :-2, 2:] + padded[..., :-2, :-2]
    )
    return -0.5 * field + 0.25 * beside + 0.125 * corners


def weigh(result, field, real_part, imag_part):
    return jnp.stack(
        [
            result[:, 0] + (real_part * field[:, 0] - imag_part * field[:, 1]),
            result[:, 1] + (real_part * field[:, 1] + imag_part * field[:, 0]),
            result[:, 2] + (real_part * field[:, 2] + imag_part * field[:, 3]),
            result[:, 3] + (real_part * field[:, 3] - imag_part * field[:, 2]),
        ],
        axis=1,
    )


def correlate(fields):
    total = jnp.zeros(fields.shape[2:], jnp.float32)
    for freq_index in range(fields.shape[0]):
        total = total + (
            fields[freq_index, 0] * fields[freq_index, 2]
            + fields[freq_index, 1] * fields[freq_index, 3]
        )
    return total


def tile_halo(sending, rim_width):
    return extended(sending, (("depth", 4), ("strip", 3)), rim_width)


def clip_domain(field, rim_width):
    row_count = field.shape[-2] - 2 * rim_width
    row_ids = (
        lax.axis_index("strip") * row_count
        - rim_width
        + jnp.arange(field.shape[-2], dtype=jnp.int32)
    )
    keep = ((row_ids >= 0) & (row_ids < row_count * lax.axis_size("strip")))[:, None]
    col_count = field.shape[-1] - 2 * rim_width
    col_ids = (
        lax.axis_index("depth") * col_count
        - rim_width
        + jnp.arange(field.shape[-1], dtype=jnp.int32)
    )
    keep = keep & ((col_ids >= 0) & (col_ids < col_count * lax.axis_size("depth")))[None, :]
    return jnp.where(keep, field, 0.0)


def chebyshev(fields, onehot, table_part, rim_width, widen):
    row_count = fields.shape[-2]
    col_count = fields.shape[-1]

    def coefficients(degree):
        pair = jnp.einsum(
            "cij,fcp->fpij", onehot, table_part[:, :, :, degree], precision=lax.Precision.HIGHEST
        )
        return (pair[:, 0], pair[:, 1])

    real_part, imag_part = coefficients(0)
    result = weigh(jnp.zeros_like(fields), fields, real_part, imag_part)
    sending = fields[None]
    widened = widen(sending, rim_width)
    wide_prev = widened[0]
    wide_curr = widened[-1]
    for inner_pass in range(rim_width):
        degree = inner_pass
        if degree == 0:
            following = mcclellan(wide_curr)
        else:
            following = 2.0 * mcclellan(wide_curr) - wide_prev
        following = clip_domain(following, rim_width)
        wide_prev, wide_curr = (wide_curr, following)
        real_part, imag_part = coefficients(degree + 1)
        inner = wide_curr[..., rim_width : rim_width + row_count, :]
        inner = inner[..., rim_width : rim_width + col_count]
        result = weigh(result, inner, real_part, imag_part)
    return result


def body(surface, velocity_class, table):
    classes = jnp.arange(CLASSES, dtype=jnp.int32)
    rim_width = PASSES
    velocity = lax.all_to_all(velocity_class, "depth", split_axis=2, concat_axis=0, tiled=True)
    col_count = velocity.shape[2]
    fields = lax.dynamic_slice_in_dim(surface, lax.axis_index("depth") * col_count, col_count, 3)

    def descend(level_index, state_pair):
        level_fields, image = state_pair
        classes_here = lax.dynamic_index_in_dim(velocity, level_index, 0, keepdims=False)
        onehot = (classes_here[None] == classes[:, None, None]).astype(jnp.float32)
        level_fields = chebyshev(level_fields, onehot, table, rim_width, tile_halo)
        image = lax.dynamic_update_index_in_dim(image, correlate(level_fields), level_index, 0)
        return (level_fields, image)

    initial = (fields, jnp.zeros((velocity.shape[0], velocity.shape[1], col_count), jnp.float32))
    fields, image = lax.fori_loop(0, velocity.shape[0], descend, initial)
    return lax.all_to_all(image, "depth", split_axis=0, concat_axis=2, tiled=True)


def pick(block, index):
    return jnp.take_along_axis(block, index, axis=1, mode="promise_in_bounds")


def interleaved(blocks):
    count = len(blocks)
    lane = lax.broadcasted_iota(jnp.int32, (SUBLANES, LANES), 1)
    found = []
    for j in range(count):
        index = lax.rem(lane * count + j, LANES)
        tile = pick(blocks[0], index)
        for n in range(1, count):
            tile = jnp.where(lane * count >= n * LANES, pick(blocks[n], index), tile)
        found.append(tile)
    return found


def restored(blocks):
    count = len(blocks)
    lane = lax.broadcasted_iota(jnp.int32, (SUBLANES, LANES), 1)
    found = []
    for n in range(count):
        index = (lane + n * LANES) // count
        tile = pick(blocks[0], index)
        for j in range(1, count):
            tile = jnp.where(lax.rem(lane, count) == j, pick(blocks[j], index), tile)
        found.append(tile)
    return found


def column_sum(tiles, lane, sub):
    right = pltpu.roll(tiles[-1], 1, axis=2)
    left = pltpu.roll(tiles[0], LANES - 1, axis=2)
    before = jnp.where(sub < 2, 0.0, pltpu.roll(right, 2, axis=1))
    after = jnp.where(sub < SUBLANES - 2, pltpu.roll(left, SUBLANES - 2, axis=1), 0.0)
    line = [jnp.where(lane == 0, before, right)] + tiles + [jnp.where(lane == LANES - 1, after, left)]
    pairs = [p + q for p, q in zip(line[:-1], line[1:])]
    return [p + q for p, q in zip(pairs[:-1], pairs[1:])]


def migrate(strips, surface_ref, velocity_ref, table_ref, own_ref, got_ref, *scratch):
    raw, classes, numbers, coef, spot, part, mixed = scratch[:7]
    per_group = PASSES + 3
    held = [scratch[7 + g * per_group : 7 + (g + 1) * per_group] for g in range(2)]
    load_sem, rim_send, rim_recv, swap_send, swap_recv = scratch[7 + 2 * per_group :]
    first = [h[0] for h in held]
    second = [h[1] for h in held]
    paired = [h[2] for h in held]
    terms = [[[first, second][level][g]] + list(held[g][3:]) for g in range(2) for level in range(2)]

    def term(g, level):
        return terms[2 * g + level]

    rows, full = velocity_ref.shape
    wide = full // QUARTERS
    rim = PASSES
    tall = rows + 2 * rim
    step = lax.axis_index("depth")
    strip = lax.axis_index("strip")
    other = 1 - step
    has_up = strip > 0
    has_down = strip < strips - 1
    no_up = jnp.logical_not(has_up)
    no_down = jnp.logical_not(has_down)
    lane = lax.broadcasted_iota(jnp.int32, (SUBLANES, LANES), 1)
    sub = lax.broadcasted_iota(jnp.int32, (SUBLANES, LANES), 0)
    tiles = range(0, wide, LANES)

    load_surface = pltpu.make_async_copy(surface_ref.at[step], raw, load_sem.at[0])
    load_classes = pltpu.make_async_copy(velocity_ref, classes.at[step], load_sem.at[1])
    load_table = pltpu.make_async_copy(table_ref, numbers, load_sem.at[2])
    load_surface.start()
    load_classes.start()
    load_table.start()

    barrier = pltpu.get_barrier_semaphore()
    pl.semaphore_signal(barrier, inc=1, device_id={"depth": other}, device_id_type=MESH)

    @pl.when(has_up)
    def _():
        pl.semaphore_signal(barrier, inc=1, device_id={"strip": strip - 1}, device_id_type=MESH)

    @pl.when(has_down)
    def _():
        pl.semaphore_signal(barrier, inc=1, device_id={"strip": strip + 1}, device_id_type=MESH)

    load_surface.wait()
    for g in range(2):
        for r in range(0, rows, SUBLANES):
            parts = [
                interleaved(
                    [
                        raw[2 * g + c, r : r + SUBLANES, q * wide + i : q * wide + i + LANES]
                        for i in tiles
                    ]
                )
                for q in range(QUARTERS)
                for c in range(2)
            ]
            for j, i in enumerate(tiles):
                block = jnp.stack([part_tiles[j] for part_tiles in parts])
                first[g][rim + r : rim + r + SUBLANES, :, i : i + LANES] = jnp.swapaxes(block, 0, 1)

    load_classes.wait()
    pl.semaphore_wait(barrier, 1 + has_up.astype(jnp.int32) + has_down.astype(jnp.int32))

    def rims(g, level):
        base = term(g, level)[0]
        up = pltpu.make_async_remote_copy(
            src_ref=base.at[pl.ds(rim, rim)],
            dst_ref=base.at[pl.ds(rim + rows, rim)],
            send_sem=rim_send.at[g, level, 0],
            recv_sem=rim_recv.at[g, level, 0],
            device_id={"strip": strip - 1},
            device_id_type=MESH,
        )
        down = pltpu.make_async_remote_copy(
            src_ref=base.at[pl.ds(rows, rim)],
            dst_ref=base.at[pl.ds(0, rim)],
            send_sem=rim_send.at[g, level, 1],
            recv_sem=rim_recv.at[g, level, 1],
            device_id={"strip": strip + 1},
            device_id_type=MESH,
        )
        return up, down

    def await_rims(g, level):
        up, down = rims(g, level)
        pl.when(has_up)(down.wait_recv)
        pl.when(has_down)(up.wait_recv)

    def zero_rims(level):
        @pl.when(no_up)
        def _():
            for g in range(2):
                term(g, level)[0][:rim] = jnp.zeros((rim, SUBLANES, wide), jnp.float32)

        @pl.when(no_down)
        def _():
            for g in range(2):
                term(g, level)[0][rim + rows :] = jnp.zeros((rim, SUBLANES, wide), jnp.float32)

    def swap_image(level, piece):
        here = pl.ds(piece * (rows // 2), rows // 2)
        return pltpu.make_async_remote_copy(
            src_ref=part.at[level, here],
            dst_ref=got_ref.at[here],
            send_sem=swap_send.at[1 + piece],
            recv_sem=swap_recv.at[1 + piece],
            device_id={"depth": other},
            device_id_type=MESH,
        )

    for g in range(2):
        up, down = rims(g, 0)
        pl.when(has_up)(up.start)
        pl.when(has_down)(down.start)
    swap_classes = pltpu.make_async_remote_copy(
        src_ref=classes.at[step],
        dst_ref=classes.at[step],
        send_sem=swap_send.at[0],
        recv_sem=swap_recv.at[0],
        device_id={"depth": other},
        device_id_type=MESH,
    )
    swap_classes.start()
    zero_rims(0)
    zero_rims(1)

    sign = jnp.where(lax.rem(sub, 2) == 1, -1.0, 1.0)
    load_table.wait()

    def fill(degree, carry):
        for p in range(2):
            spread = jnp.zeros((SUBLANES, LANES), jnp.float32)
            for c in range(CLASSES):
                spread = jnp.where(lane == c, numbers[step, c, p, degree], spread)
            coef[p, degree] = spread * sign if p else spread
        return carry

    lax.fori_loop(0, PASSES + 1, fill, 0)

    def look_up(level):
        for r in range(0, rows, SUBLANES):
            for q in range(QUARTERS):
                found = interleaved(
                    [
                        classes[level, r : r + SUBLANES, q * wide + i : q * wide + i + LANES]
                        for i in tiles
                    ]
                )
                for i, tile in zip(tiles, found):
                    mixed[r : r + SUBLANES, q * wide + i : q * wide + i + LANES] = tile

        def block(b, carry):
            for j in range(4):
                r = b * 4 + j
                kind = mixed[pl.ds(r, 1), :]
                for i in tiles:
                    index = None
                    for q in range(QUARTERS):
                        at = q * wide + i
                        spread = jnp.broadcast_to(kind[:, at : at + LANES], (SUBLANES, LANES))
                        index = spread if q == 0 else jnp.where(sub < 2 * q, index, spread)
                    for p in range(2):
                        for k in range(PASSES + 1):
                            spot[p, k, r, :, i : i + LANES] = jnp.take_along_axis(
                                coef[p, k], index, axis=1, mode="promise_in_bounds"
                            )
            return carry

        lax.fori_loop(0, rows // 4, block, 0)

    results = (second, paired)

    def weigh(g, level, low, high):
        series = term(g, level)
        for r in range(low, high, 4):
            size = min(4, high - r)
            even = lax.rem(lax.broadcasted_iota(jnp.int32, (size, SUBLANES, LANES), 1), 2) == 0
            for i in tiles:
                same = cross = None
                for k in range(PASSES + 1):
                    field = series[k][rim + r : rim + r + size, :, i : i + LANES]
                    real = spot[0, k, r : r + size, :, i : i + LANES] * field
                    imag = spot[1, k, r : r + size, :, i : i + LANES] * field
                    same = real if same is None else same + real
                    cross = imag if cross is None else cross + imag
                cross = jnp.where(
                    even, pltpu.roll(cross, SUBLANES - 1, axis=1), pltpu.roll(cross, 1, axis=1)
                )
                results[level][g][rim + r : rim + r + size, :, i : i + LANES] = (
                    same - cross if g else same + cross
                )

    def correlate_step(level, low, high):
        for r in range(low, high, SUBLANES):
            products = []
            for i in tiles:
                source, receiver = (
                    results[level][g][rim + r : rim + r + SUBLANES, :, i : i + LANES] for g in range(2)
                )
                products.append(jnp.swapaxes(source * receiver, 0, 1))
            for q in range(QUARTERS):
                found = restored([p[2 * q] + p[2 * q + 1] for p in products])
                for i, tile in zip(tiles, found):
                    part[level, r : r + SUBLANES, q * wide + i : q * wide + i + LANES] = tile

    def groups(low, high):
        count = max(1, -(-(high - low) // 5))
        found, at = [], low
        for n in range(count):
            size = (high - at) // (count - n)
            found.append((at, size))
            at += size
        return found

    def sweep(g, level, degree, spans):
        source, target = term(g, level)[degree - 1], term(g, level)[degree]
        for at, size in spans:
            lanes = lax.broadcasted_iota(jnp.int32, (size, SUBLANES, LANES), 2)
            subs = lax.broadcasted_iota(jnp.int32, (size, SUBLANES, LANES), 1)
            sums = []
            inner = []
            for i in tiles:
                field = source[at - 1 : at + size + 1, :, i : i + LANES]
                pair = field[:-1] + field[1:]
                sums.append(pair[:-1] + pair[1:])
                inner.append(field[1:-1])
            for i, total, field in zip(tiles, column_sum(sums, lanes, subs), inner):
                if degree == 1:
                    joint = 0.125 * total
                else:
                    joint = 0.25 * total - paired[g][at : at + size, :, i : i + LANES]
                if degree < PASSES:
                    paired[g][at : at + size, :, i : i + LANES] = joint
                value = joint - field
                for edge, absent in ((rim - 1, no_up), (rim + rows, no_down)):
                    if at <= edge < at + size:
                        lines = [value[row : row + 1] for row in range(size)]
                        lines[edge - at] = jnp.where(absent, 0.0, lines[edge - at])
                        value = jnp.concatenate(lines, axis=0)
                target[at : at + size, :, i : i + LANES] = value

    def inside(g, level, degree):
        low, high = rim + degree, rim + rows - degree
        if degree < PASSES and low < high:
            sweep(g, level, degree, groups(low, high))

    def outside(g, level, degree):
        if degree == PASSES:
            return sweep(g, level, degree, groups(rim, rim + rows))
        middle = tall // 2
        above = groups(degree, min(rim + degree, middle))
        below = groups(max(rim + rows - degree, middle), tall - degree)
        sweep(g, level, degree, [span for both in zip(above, below) for span in both])

    degrees = range(1, PASSES + 1)
    for degree in degrees:
        inside(0, 0, degree)
        inside(1, 0, degree)
    swap_classes.wait_recv()
    look_up(0)
    for g in range(2):
        await_rims(g, 0)
        for degree in degrees:
            outside(g, 0, degree)
            if g == 1:
                inside(0, 1, degree)
        up, down = rims(g, 1)
        weigh(g, 0, 0, rim)
        pl.when(has_up)(up.start)
        weigh(g, 0, rim, rows)
        pl.when(has_down)(down.start)

    look_up(1)
    correlate_step(0, 0, rows)

    @pl.when(step == 1)
    def _():
        swap_image(0, 0).start()
        swap_image(0, 1).start()

    @pl.when(step == 0)
    def _():
        pltpu.make_async_copy(part.at[0], own_ref, load_sem.at[3]).start()

    await_rims(0, 1)
    for degree in degrees:
        outside(0, 1, degree)
        inside(1, 1, degree)
    weigh(0, 1, 0, rows)
    await_rims(1, 1)
    for degree in degrees:
        outside(1, 1, degree)
    half = rows // 2
    for piece in range(2):
        weigh(1, 1, piece * half, (piece + 1) * half)
        correlate_step(1, piece * half, (piece + 1) * half)

        @pl.when(step == 0)
        def _(piece=piece):
            swap_image(1, piece).start()

    @pl.when(step == 1)
    def _():
        pltpu.make_async_copy(part.at[1], own_ref, load_sem.at[3]).start()

    for piece in range(2):
        swap_image(0, piece).wait_send()
        swap_image(0, piece).wait_recv()
    pltpu.make_async_copy(part.at[0], own_ref, load_sem.at[3]).wait()
    swap_classes.wait_send()
    for g in range(2):
        for level in range(2):
            up, down = rims(g, level)
            pl.when(has_up)(up.wait_send)
            pl.when(has_down)(down.wait_send)


def in_kernel(strips, surface, velocity_class, table):
    freqs, parts, rows, full = surface.shape
    wide = full // QUARTERS
    tall = rows + 2 * PASSES
    f32 = jnp.float32
    fields = pltpu.VMEM((tall, SUBLANES, wide), f32)
    own, got = pl.pallas_call(
        functools.partial(migrate, strips),
        out_shape=[jax.ShapeDtypeStruct((rows, full), f32)] * 2,
        in_specs=[pl.BlockSpec(memory_space=pl.ANY)] * 3,
        out_specs=[pl.BlockSpec(memory_space=pl.ANY)] * 2,
        scratch_shapes=[
            pltpu.VMEM((parts, rows, full), f32),
            pltpu.VMEM((2, rows, full), jnp.int32),
            pltpu.SMEM(table.shape, f32),
            pltpu.VMEM((2, PASSES + 1, SUBLANES, LANES), f32),
            pltpu.VMEM((2, PASSES + 1, rows, SUBLANES, wide), f32),
            pltpu.VMEM((2, rows, full), f32),
            pltpu.VMEM((rows, full), jnp.int32),
        ]
        + [fields] * (2 * (PASSES + 3))
        + [
            pltpu.SemaphoreType.DMA((4,)),
            pltpu.SemaphoreType.DMA((2, 2, 2)),
            pltpu.SemaphoreType.DMA((2, 2, 2)),
            pltpu.SemaphoreType.DMA((3,)),
            pltpu.SemaphoreType.DMA((3,)),
        ],
        compiler_params=pltpu.CompilerParams(
            collective_id=0, has_side_effects=True, vmem_limit_bytes=56 * 2**20
        ),
    )(surface, velocity_class.reshape(rows, full), table)
    return (own + got)[None]


def fits(mesh, surface, velocity_class):
    freqs, parts, rows, full = surface.shape
    return (
        mesh.shape["depth"] == 2
        and velocity_class.shape[0] == 1
        and freqs == 2
        and parts == 4
        and rows % (2 * SUBLANES) == 0
        and PASSES <= rows < 2 * PASSES
        and full % (QUARTERS * LANES) == 0
        and LANES % (full // (QUARTERS * LANES)) == 0
        and rows * full <= 2**15
    )


def solution(mesh):
    in_specs = (P(None, None, "strip", None), P("depth", "strip", None), P())
    out_specs = P("depth", "strip", None)

    def part(surface, velocity_class, table):
        if fits(mesh, surface, velocity_class):
            return in_kernel(mesh.shape["strip"], surface, velocity_class, table)
        return body(surface, velocity_class, table)

    return jax.shard_map(part, mesh=mesh, in_specs=in_specs, out_specs=out_specs, check_vma=False)
```

```python
import functools

import jax
import jax.numpy as jnp
from jax import lax
from jax.experimental import pallas as pl
from jax.experimental.pallas import tpu as pltpu
from jax.sharding import PartitionSpec as P

PASSES = 9
CLASSES = 8
LANES = 128
SUBLANES = 8
QUARTERS = 4
MESH = pl.DeviceIdType.MESH


def extended(shard, sides, width):
    for axis, dim in sides:
        devices, length = (lax.axis_size(axis), shard.shape[dim])
        up = [(i, (i + 1) % devices) for i in range(devices - 1)]
        down = [(j, i) for i, j in up]
        last = lax.slice_in_dim(shard, length - width, length, axis=dim)
        initial = lax.slice_in_dim(shard, 0, width, axis=dim)
        before = lax.ppermute(last, axis, up)
        after = lax.ppermute(initial, axis, down)
        shard = jnp.concatenate([before, shard, after], axis=dim)
    return shard


def mcclellan(field):
    lead = [(0, 0)] * (field.ndim - 2)
    padded = jnp.pad(field, lead + [(1, 1), (1, 1)])
    beside = (
        padded[..., 2:, 1:-1]
        + padded[..., :-2, 1:-1]
        + padded[..., 1:-1, 2:]
        + padded[..., 1:-1, :-2]
    )
    corners = (
        padded[..., 2:, 2:] + padded[..., 2:, :-2] + padded[..., :-2, 2:] + padded[..., :-2, :-2]
    )
    return -0.5 * field + 0.25 * beside + 0.125 * corners


def weigh(result, field, real_part, imag_part):
    return jnp.stack(
        [
            result[:, 0] + (real_part * field[:, 0] - imag_part * field[:, 1]),
            result[:, 1] + (real_part * field[:, 1] + imag_part * field[:, 0]),
            result[:, 2] + (real_part * field[:, 2] + imag_part * field[:, 3]),
            result[:, 3] + (real_part * field[:, 3] - imag_part * field[:, 2]),
        ],
        axis=1,
    )


def correlate(fields):
    total = jnp.zeros(fields.shape[2:], jnp.float32)
    for freq_index in range(fields.shape[0]):
        total = total + (
            fields[freq_index, 0] * fields[freq_index, 2]
            + fields[freq_index, 1] * fields[freq_index, 3]
        )
    return total


def tile_halo(sending, rim_width):
    return extended(sending, (("depth", 4), ("strip", 3)), rim_width)


def clip_domain(field, rim_width):
    row_count = field.shape[-2] - 2 * rim_width
    row_ids = (
        lax.axis_index("strip") * row_count
        - rim_width
        + jnp.arange(field.shape[-2], dtype=jnp.int32)
    )
    keep = ((row_ids >= 0) & (row_ids < row_count * lax.axis_size("strip")))[:, None]
    col_count = field.shape[-1] - 2 * rim_width
    col_ids = (
        lax.axis_index("depth") * col_count
        - rim_width
        + jnp.arange(field.shape[-1], dtype=jnp.int32)
    )
    keep = keep & ((col_ids >= 0) & (col_ids < col_count * lax.axis_size("depth")))[None, :]
    return jnp.where(keep, field, 0.0)


def chebyshev(fields, onehot, table_part, rim_width, widen):
    row_count = fields.shape[-2]
    col_count = fields.shape[-1]

    def coefficients(degree):
        pair = jnp.einsum(
            "cij,fcp->fpij", onehot, table_part[:, :, :, degree], precision=lax.Precision.HIGHEST
        )
        return (pair[:, 0], pair[:, 1])

    real_part, imag_part = coefficients(0)
    result = weigh(jnp.zeros_like(fields), fields, real_part, imag_part)
    sending = fields[None]
    widened = widen(sending, rim_width)
    wide_prev = widened[0]
    wide_curr = widened[-1]
    for inner_pass in range(rim_width):
        degree = inner_pass
        if degree == 0:
            following = mcclellan(wide_curr)
        else:
            following = 2.0 * mcclellan(wide_curr) - wide_prev
        following = clip_domain(following, rim_width)
        wide_prev, wide_curr = (wide_curr, following)
        real_part, imag_part = coefficients(degree + 1)
        inner = wide_curr[..., rim_width : rim_width + row_count, :]
        inner = inner[..., rim_width : rim_width + col_count]
        result = weigh(result, inner, real_part, imag_part)
    return result


def body(surface, velocity_class, table):
    classes = jnp.arange(CLASSES, dtype=jnp.int32)
    rim_width = PASSES
    velocity = lax.all_to_all(velocity_class, "depth", split_axis=2, concat_axis=0, tiled=True)
    col_count = velocity.shape[2]
    fields = lax.dynamic_slice_in_dim(surface, lax.axis_index("depth") * col_count, col_count, 3)

    def descend(level_index, state_pair):
        level_fields, image = state_pair
        classes_here = lax.dynamic_index_in_dim(velocity, level_index, 0, keepdims=False)
        onehot = (classes_here[None] == classes[:, None, None]).astype(jnp.float32)
        level_fields = chebyshev(level_fields, onehot, table, rim_width, tile_halo)
        image = lax.dynamic_update_index_in_dim(image, correlate(level_fields), level_index, 0)
        return (level_fields, image)

    initial = (fields, jnp.zeros((velocity.shape[0], velocity.shape[1], col_count), jnp.float32))
    fields, image = lax.fori_loop(0, velocity.shape[0], descend, initial)
    return lax.all_to_all(image, "depth", split_axis=0, concat_axis=2, tiled=True)


def pick(block, index):
    return jnp.take_along_axis(block, index, axis=1, mode="promise_in_bounds")


def interleaved(blocks):
    count = len(blocks)
    lane = lax.broadcasted_iota(jnp.int32, (SUBLANES, LANES), 1)
    found = []
    for j in range(count):
        index = lax.rem(lane * count + j, LANES)
        tile = pick(blocks[0], index)
        for n in range(1, count):
            tile = jnp.where(lane * count >= n * LANES, pick(blocks[n], index), tile)
        found.append(tile)
    return found


def restored(blocks):
    count = len(blocks)
    lane = lax.broadcasted_iota(jnp.int32, (SUBLANES, LANES), 1)
    found = []
    for n in range(count):
        index = (lane + n * LANES) // count
        tile = pick(blocks[0], index)
        for j in range(1, count):
            tile = jnp.where(lax.rem(lane, count) == j, pick(blocks[j], index), tile)
        found.append(tile)
    return found


def column_sum(tiles, lane, sub):
    right = pltpu.roll(tiles[-1], 1, axis=2)
    left = pltpu.roll(tiles[0], LANES - 1, axis=2)
    before = jnp.where(sub < 2, 0.0, pltpu.roll(right, 2, axis=1))
    after = jnp.where(sub < SUBLANES - 2, pltpu.roll(left, SUBLANES - 2, axis=1), 0.0)
    line = [jnp.where(lane == 0, before, right)] + tiles + [jnp.where(lane == LANES - 1, after, left)]
    pairs = [p + q for p, q in zip(line[:-1], line[1:])]
    return [p + q for p, q in zip(pairs[:-1], pairs[1:])]


def migrate(strips, surface_ref, velocity_ref, table_ref, own_ref, got_ref, *scratch):
    raw, classes, numbers, coef, spot, part, mixed = scratch[:7]
    per_group = PASSES + 3
    held = [scratch[7 + g * per_group : 7 + (g + 1) * per_group] for g in range(2)]
    load_sem, rim_send, rim_recv, swap_send, swap_recv = scratch[7 + 2 * per_group :]
    first = [h[0] for h in held]
    second = [h[1] for h in held]
    paired = [h[2] for h in held]
    terms = [[[first, second][level][g]] + list(held[g][3:]) for g in range(2) for level in range(2)]

    def term(g, level):
        return terms[2 * g + level]

    rows, full = velocity_ref.shape
    wide = full // QUARTERS
    rim = PASSES
    tall = rows + 2 * rim
    step = lax.axis_index("depth")
    strip = lax.axis_index("strip")
    other = 1 - step
    has_up = strip > 0
    has_down = strip < strips - 1
    no_up = jnp.logical_not(has_up)
    no_down = jnp.logical_not(has_down)
    lane = lax.broadcasted_iota(jnp.int32, (SUBLANES, LANES), 1)
    sub = lax.broadcasted_iota(jnp.int32, (SUBLANES, LANES), 0)
    tiles = range(0, wide, LANES)

    load_surface = pltpu.make_async_copy(surface_ref.at[step], raw, load_sem.at[0])
    load_classes = pltpu.make_async_copy(velocity_ref, classes.at[step], load_sem.at[1])
    load_table = pltpu.make_async_copy(table_ref, numbers, load_sem.at[2])
    load_surface.start()
    load_classes.start()
    load_table.start()

    barrier = pltpu.get_barrier_semaphore()
    pl.semaphore_signal(barrier, inc=1, device_id={"depth": other}, device_id_type=MESH)

    @pl.when(has_up)
    def _():
        pl.semaphore_signal(barrier, inc=1, device_id={"strip": strip - 1}, device_id_type=MESH)

    @pl.when(has_down)
    def _():
        pl.semaphore_signal(barrier, inc=1, device_id={"strip": strip + 1}, device_id_type=MESH)

    load_surface.wait()
    for g in range(2):
        for r in range(0, rows, SUBLANES):
            parts = [
                interleaved(
                    [
                        raw[2 * g + c, r : r + SUBLANES, q * wide + i : q * wide + i + LANES]
                        for i in tiles
                    ]
                )
                for q in range(QUARTERS)
                for c in range(2)
            ]
            for j, i in enumerate(tiles):
                block = jnp.stack([part_tiles[j] for part_tiles in parts])
                first[g][rim + r : rim + r + SUBLANES, :, i : i + LANES] = jnp.swapaxes(block, 0, 1)

    load_classes.wait()
    pl.semaphore_wait(barrier, 1 + has_up.astype(jnp.int32) + has_down.astype(jnp.int32))

    def rims(g, level):
        base = term(g, level)[0]
        up = pltpu.make_async_remote_copy(
            src_ref=base.at[pl.ds(rim, rim)],
            dst_ref=base.at[pl.ds(rim + rows, rim)],
            send_sem=rim_send.at[g, level, 0],
            recv_sem=rim_recv.at[g, level, 0],
            device_id={"strip": strip - 1},
            device_id_type=MESH,
        )
        down = pltpu.make_async_remote_copy(
            src_ref=base.at[pl.ds(rows, rim)],
            dst_ref=base.at[pl.ds(0, rim)],
            send_sem=rim_send.at[g, level, 1],
            recv_sem=rim_recv.at[g, level, 1],
            device_id={"strip": strip + 1},
            device_id_type=MESH,
        )
        return up, down

    def await_rims(g, level):
        up, down = rims(g, level)
        pl.when(has_up)(down.wait_recv)
        pl.when(has_down)(up.wait_recv)

    def zero_rims(level):
        @pl.when(no_up)
        def _():
            for g in range(2):
                term(g, level)[0][:rim] = jnp.zeros((rim, SUBLANES, wide), jnp.float32)

        @pl.when(no_down)
        def _():
            for g in range(2):
                term(g, level)[0][rim + rows :] = jnp.zeros((rim, SUBLANES, wide), jnp.float32)

    def swap_image(level, piece):
        here = pl.ds(piece * (rows // 2), rows // 2)
        return pltpu.make_async_remote_copy(
            src_ref=part.at[level, here],
            dst_ref=got_ref.at[here],
            send_sem=swap_send.at[1 + piece],
            recv_sem=swap_recv.at[1 + piece],
            device_id={"depth": other},
            device_id_type=MESH,
        )

    up, down = rims(0, 0)
    pl.when(has_up)(up.start)
    pl.when(has_down)(down.start)
    swap_classes = pltpu.make_async_remote_copy(
        src_ref=classes.at[step],
        dst_ref=classes.at[step],
        send_sem=swap_send.at[0],
        recv_sem=swap_recv.at[0],
        device_id={"depth": other},
        device_id_type=MESH,
    )
    swap_classes.start()
    zero_rims(0)
    zero_rims(1)

    sign = jnp.where(lax.rem(sub, 2) == 1, -1.0, 1.0)
    load_table.wait()

    def fill(degree, carry):
        for p in range(2):
            spread = jnp.zeros((SUBLANES, LANES), jnp.float32)
            for c in range(CLASSES):
                spread = jnp.where(lane == c, numbers[step, c, p, degree], spread)
            coef[p, degree] = spread * sign if p else spread
        return carry

    lax.fori_loop(0, PASSES + 1, fill, 0)

    def look_up(level):
        for r in range(0, rows, SUBLANES):
            for q in range(QUARTERS):
                found = interleaved(
                    [
                        classes[level, r : r + SUBLANES, q * wide + i : q * wide + i + LANES]
                        for i in tiles
                    ]
                )
                for i, tile in zip(tiles, found):
                    mixed[r : r + SUBLANES, q * wide + i : q * wide + i + LANES] = tile

        def block(b, carry):
            for j in range(4):
                r = b * 4 + j
                kind = mixed[pl.ds(r, 1), :]
                for i in tiles:
                    index = None
                    for q in range(QUARTERS):
                        at = q * wide + i
                        spread = jnp.broadcast_to(kind[:, at : at + LANES], (SUBLANES, LANES))
                        index = spread if q == 0 else jnp.where(sub < 2 * q, index, spread)
                    for p in range(2):
                        for k in range(PASSES + 1):
                            spot[p, k, r, :, i : i + LANES] = jnp.take_along_axis(
                                coef[p, k], index, axis=1, mode="promise_in_bounds"
                            )
            return carry

        lax.fori_loop(0, rows // 4, block, 0)

    results = (second, paired)

    def weigh(g, level, low, high):
        series = term(g, level)
        for r in range(low, high, 4):
            size = min(4, high - r)
            even = lax.rem(lax.broadcasted_iota(jnp.int32, (size, SUBLANES, LANES), 1), 2) == 0
            for i in tiles:
                same = cross = None
                for k in range(PASSES + 1):
                    field = series[k][rim + r : rim + r + size, :, i : i + LANES]
                    real = spot[0, k, r : r + size, :, i : i + LANES] * field
                    imag = spot[1, k, r : r + size, :, i : i + LANES] * field
                    same = real if same is None else same + real
                    cross = imag if cross is None else cross + imag
                cross = jnp.where(
                    even, pltpu.roll(cross, SUBLANES - 1, axis=1), pltpu.roll(cross, 1, axis=1)
                )
                results[level][g][rim + r : rim + r + size, :, i : i + LANES] = (
                    same - cross if g else same + cross
                )

    def correlate_step(level, low, high):
        for r in range(low, high, SUBLANES):
            products = []
            for i in tiles:
                source, receiver = (
                    results[level][g][rim + r : rim + r + SUBLANES, :, i : i + LANES] for g in range(2)
                )
                products.append(jnp.swapaxes(source * receiver, 0, 1))
            for q in range(QUARTERS):
                found = restored([p[2 * q] + p[2 * q + 1] for p in products])
                for i, tile in zip(tiles, found):
                    part[level, r : r + SUBLANES, q * wide + i : q * wide + i + LANES] = tile

    def groups(low, high):
        count = max(1, -(-(high - low) // 5))
        found, at = [], low
        for n in range(count):
            size = (high - at) // (count - n)
            found.append((at, size))
            at += size
        return found

    def sweep(g, level, degree, spans):
        source, target = term(g, level)[degree - 1], term(g, level)[degree]
        for at, size in spans:
            lanes = lax.broadcasted_iota(jnp.int32, (size, SUBLANES, LANES), 2)
            subs = lax.broadcasted_iota(jnp.int32, (size, SUBLANES, LANES), 1)
            sums = []
            inner = []
            for i in tiles:
                field = source[at - 1 : at + size + 1, :, i : i + LANES]
                pair = field[:-1] + field[1:]
                sums.append(pair[:-1] + pair[1:])
                inner.append(field[1:-1])
            for i, total, field in zip(tiles, column_sum(sums, lanes, subs), inner):
                if degree == 1:
                    joint = 0.125 * total
                else:
                    joint = 0.25 * total - paired[g][at : at + size, :, i : i + LANES]
                if degree < PASSES:
                    paired[g][at : at + size, :, i : i + LANES] = joint
                value = joint - field
                for edge, absent in ((rim - 1, no_up), (rim + rows, no_down)):
                    if at <= edge < at + size:
                        lines = [value[row : row + 1] for row in range(size)]
                        lines[edge - at] = jnp.where(absent, 0.0, lines[edge - at])
                        value = jnp.concatenate(lines, axis=0)
                target[at : at + size, :, i : i + LANES] = value

    def inside(g, level, degree):
        low, high = rim + degree, rim + rows - degree
        if degree < PASSES and low < high:
            sweep(g, level, degree, groups(low, high))

    def outside(g, level, degree):
        if degree == PASSES:
            return sweep(g, level, degree, groups(rim, rim + rows))
        middle = tall // 2
        above = groups(degree, min(rim + degree, middle))
        below = groups(max(rim + rows - degree, middle), tall - degree)
        sweep(g, level, degree, [span for both in zip(above, below) for span in both])

    degrees = range(1, PASSES + 1)
    up, down = rims(0, 0)
    pl.when(has_up)(up.wait_send)
    pl.when(has_down)(down.wait_send)
    up, down = rims(1, 0)
    pl.when(has_up)(up.start)
    pl.when(has_down)(down.start)
    for degree in degrees:
        inside(0, 0, degree)
        inside(1, 0, degree)
    swap_classes.wait_recv()
    look_up(0)
    for g in range(2):
        await_rims(g, 0)
        for degree in degrees:
            outside(g, 0, degree)
            if g == 1:
                inside(0, 1, degree)
        up, down = rims(g, 1)
        weigh(g, 0, 0, rim)
        pl.when(has_up)(up.start)
        weigh(g, 0, rim, rows)
        pl.when(has_down)(down.start)

    look_up(1)
    correlate_step(0, 0, rows)

    @pl.when(step == 1)
    def _():
        swap_image(0, 0).start()
        swap_image(0, 1).start()

    @pl.when(step == 0)
    def _():
        pltpu.make_async_copy(part.at[0], own_ref, load_sem.at[3]).start()

    await_rims(0, 1)
    for degree in degrees:
        outside(0, 1, degree)
        inside(1, 1, degree)
    weigh(0, 1, 0, rows)
    await_rims(1, 1)
    for degree in degrees:
        outside(1, 1, degree)
    half = rows // 2
    for piece in range(2):
        weigh(1, 1, piece * half, (piece + 1) * half)
        correlate_step(1, piece * half, (piece + 1) * half)

        @pl.when(step == 0)
        def _(piece=piece):
            swap_image(1, piece).start()

    @pl.when(step == 1)
    def _():
        pltpu.make_async_copy(part.at[1], own_ref, load_sem.at[3]).start()

    for piece in range(2):
        swap_image(0, piece).wait_send()
        swap_image(0, piece).wait_recv()
    pltpu.make_async_copy(part.at[0], own_ref, load_sem.at[3]).wait()
    swap_classes.wait_send()
    for g, level in ((1, 0), (0, 1), (1, 1)):
        up, down = rims(g, level)
        pl.when(has_up)(up.wait_send)
        pl.when(has_down)(down.wait_send)


def in_kernel(strips, surface, velocity_class, table):
    freqs, parts, rows, full = surface.shape
    wide = full // QUARTERS
    tall = rows + 2 * PASSES
    f32 = jnp.float32
    fields = pltpu.VMEM((tall, SUBLANES, wide), f32)
    own, got = pl.pallas_call(
        functools.partial(migrate, strips),
        out_shape=[jax.ShapeDtypeStruct((rows, full), f32)] * 2,
        in_specs=[pl.BlockSpec(memory_space=pl.ANY)] * 3,
        out_specs=[pl.BlockSpec(memory_space=pl.ANY)] * 2,
        scratch_shapes=[
            pltpu.VMEM((parts, rows, full), f32),
            pltpu.VMEM((2, rows, full), jnp.int32),
            pltpu.SMEM(table.shape, f32),
            pltpu.VMEM((2, PASSES + 1, SUBLANES, LANES), f32),
            pltpu.VMEM((2, PASSES + 1, rows, SUBLANES, wide), f32),
            pltpu.VMEM((2, rows, full), f32),
            pltpu.VMEM((rows, full), jnp.int32),
        ]
        + [fields] * (2 * (PASSES + 3))
        + [
            pltpu.SemaphoreType.DMA((4,)),
            pltpu.SemaphoreType.DMA((2, 2, 2)),
            pltpu.SemaphoreType.DMA((2, 2, 2)),
            pltpu.SemaphoreType.DMA((3,)),
            pltpu.SemaphoreType.DMA((3,)),
        ],
        compiler_params=pltpu.CompilerParams(
            collective_id=0, has_side_effects=True, vmem_limit_bytes=56 * 2**20
        ),
    )(surface, velocity_class.reshape(rows, full), table)
    return (own + got)[None]


def fits(mesh, surface, velocity_class):
    freqs, parts, rows, full = surface.shape
    return (
        mesh.shape["depth"] == 2
        and velocity_class.shape[0] == 1
        and freqs == 2
        and parts == 4
        and rows % (2 * SUBLANES) == 0
        and PASSES <= rows < 2 * PASSES
        and full % (QUARTERS * LANES) == 0
        and LANES % (full // (QUARTERS * LANES)) == 0
        and rows * full <= 2**15
    )


def solution(mesh):
    in_specs = (P(None, None, "strip", None), P("depth", "strip", None), P())
    out_specs = P("depth", "strip", None)

    def part(surface, velocity_class, table):
        if fits(mesh, surface, velocity_class):
            return in_kernel(mesh.shape["strip"], surface, velocity_class, table)
        return body(surface, velocity_class, table)

    return jax.shard_map(part, mesh=mesh, in_specs=in_specs, out_specs=out_specs, check_vma=False)
```
